32 devices in a mesh: section: 4 (over z), dp: 4 (over x, core), mp: 2 (over y).
Axes of the slice: x: 2, y: 2, z: 4, core: 2. Of those that a mesh axis runs over, the one named last changes fastest.
Arguments:
- section_in: bfloat16 [2, 4, 256, 12288], P(None, 'section', 'dp'), may hold values from -6 to 6
- out_grad: bfloat16 [2, 4, 256, 12288], P(None, 'section', 'dp'), may hold values from -1.5 to 1.5
- lengths: int32 [2, 4, 4], P(None, 'section', 'dp'), may hold values from 1 to 64, as said below
- w_in: bfloat16 [4, 2, 192, 128, 128], P('section', None, 'mp'), as said below
- w_out: bfloat16 [4, 2, 192, 128, 128], P('section', None, 'mp'), as said below
- idx_in: int32 [4, 2, 192], P('section', None, 'mp'), may hold values from 0 to 95, as said below
- idx_out: int32 [4, 2, 192], P('section', None, 'mp'), may hold values from 0 to 95, as said below
Outputs:
- passed: bfloat16 [2, 4, 256, 12288], P(None, 'section', ('dp', 'mp'))
- grads: float32 [4, 2, 2, 96, 128, 128], P(None, None, 'mp', 'section', 'dp')
The draws below stay inside these ranges and needn't reach their ends.
Inputs may be any that keep to these rules, and one draw needn't show every extreme that they name: `lengths`: some micro-batch is full and some has a single live row. w_in[s, 1] equals w_in[3 - s, 0]: copy 1 at section s is the up relay's replica of layer 3 - s. w_out[s, 1] equals w_out[3 - s, 0]. idx_in[s, 1] equals idx_in[3 - s, 0]. idx_out[s, 1] equals idx_out[3 - s, 0].
All inputs are finite; a program needn't handle non-finite values.
Results may differ from the reference program's by a relative error of at most 0.0095.
Values may be sent and summed in bfloat16 or wider, within the bound.
No kernel may reach another device: no remote copies, remote signals or barrier semaphores. Data moves between devices by JAX's collectives and lax.ppermute only.
A program may use at most 128 MiB of HBM per device.

```python
import math
import jax
import jax.numpy as jnp
from jax import lax

D = 12288
BLK = 128
MB = 64
SECTIONS = 4
REPLICAS = 4
TOKENS = 256
FBT = 192
FB_DEV = 96
N_MP = 2


def draw_w_in(key, part):
    inner = jax.random.fold_in(key, 11)
    base = jax.random.normal(inner, (SECTIONS, FBT, BLK, BLK), jnp.float32)
    base = base * (1.0 / math.sqrt(BLK))
    return jnp.stack([base, jnp.flip(base, 0)], axis=1).astype(jnp.bfloat16)


def draw_w_out(key, part):
    inner = jax.random.fold_in(key, 12)
    base = jax.random.normal(inner, (SECTIONS, FBT, BLK, BLK), jnp.float32)
    base = base * (1.0 / math.sqrt(BLK * max(1, FBT // (D // BLK))))
    return jnp.stack([base, jnp.flip(base, 0)], axis=1).astype(jnp.bfloat16)


def draw_idx_in(key, part):
    base = jax.random.randint(jax.random.fold_in(key, 13), (SECTIONS, FBT), 0, D // BLK, jnp.int32)
    return jnp.stack([base, jnp.flip(base, 0)], axis=1)


def draw_idx_out(key, part):
    base = jax.random.randint(jax.random.fold_in(key, 14), (SECTIONS, FBT), 0, D // BLK, jnp.int32)
    return jnp.stack([base, jnp.flip(base, 0)], axis=1)


def draw_lengths(key, part):
    drawn = jax.random.randint(jax.random.fold_in(key, 15), (2, SECTIONS, REPLICAS), 1, MB + 1, jnp.int32)
    return drawn.at[0, 0, 0].set(MB).at[1, -1, -1].set(1)


def shard_levels(own_key, dims, split, smallest, largest):
    def one(axis_at, shards_of):
        steps = jax.random.uniform(jax.random.fold_in(jax.random.fold_in(own_key, 6), axis_at), (shards_of,), jnp.float32, smallest / len(split), largest / len(split))
        return jnp.repeat(jnp.exp(steps), dims[axis_at] // shards_of).reshape((-1,) + (1,) * (len(dims) - axis_at - 1))

    factor_of = one(*split[0])
    for cut in split[1:]:
        factor_of = factor_of * one(*cut)
    return factor_of


def normal_values(stream_key, shape, width, bound, pieces=(), kind=jnp.bfloat16):
    level = shard_levels(stream_key, shape, pieces, -0.22, 0.18) if pieces else 1.0
    values = jax.random.normal(stream_key, shape, jnp.float32) * width * level
    return jnp.minimum(jnp.maximum(values, -bound), bound).astype(kind)


def setup_inputs(seed: int = 0) -> dict:
    keys = jax.random.split(jax.random.key(seed), 8)
    section_in = normal_values(keys[0], (2, SECTIONS, TOKENS, D), 1.0, 6.0, ((1, 4), (2, 4)))
    out_grad = normal_values(keys[1], (2, SECTIONS, TOKENS, D), 0.25, 1.5, ((1, 4), (2, 4)))
    lengths = draw_lengths(jax.random.fold_in(keys[7], 71), 0)
    w_in = draw_w_in(jax.random.fold_in(keys[7], 71), 0)
    w_out = draw_w_out(jax.random.fold_in(keys[7], 71), 0)
    idx_in = draw_idx_in(jax.random.fold_in(keys[7], 71), 0)
    idx_out = draw_idx_out(jax.random.fold_in(keys[7], 71), 0)
    return {"section_in": section_in, "out_grad": out_grad, "lengths": lengths, "w_in": w_in, "w_out": w_out, "idx_in": idx_in, "idx_out": idx_out}


def gelu_back(pre, upstream):
    return jax.vjp(lambda value: jax.nn.gelu(value, approximate=True), pre)[1](upstream)[0]

def section_pass(operands):
    inputs, masked, weight_in, weight_out, index_in, index_out = operands
    count = D // BLK
    in_blocks = inputs.reshape(TOKENS, count, BLK)
    back_blocks = masked.reshape(TOKENS, count, BLK)
    picked = jnp.take(in_blocks, index_in, axis=1)
    back = jnp.take(back_blocks, index_out, axis=1)
    pre = jnp.einsum('tjc,jcd->tjd', picked.astype(jnp.float32), weight_in.astype(jnp.float32))
    act = jax.nn.gelu(pre, approximate=True).astype(jnp.bfloat16)
    back_pre = jnp.einsum('tjd,jcd->tjc', back.astype(jnp.float32), weight_out.astype(jnp.float32))
    grad_pre = gelu_back(pre, back_pre).astype(jnp.bfloat16)
    terms = jnp.einsum('tjd,jcd->tjc', grad_pre.astype(jnp.float32), weight_in.astype(jnp.float32))
    terms = terms.reshape(TOKENS, N_MP, FB_DEV, BLK)
    onehot = jax.nn.one_hot(index_in.reshape(N_MP, FB_DEV), count, dtype=jnp.float32)
    share = jnp.einsum('tmjc,mjb->tmbc', terms, onehot, precision=lax.Precision.HIGHEST).astype(jnp.bfloat16)
    summed = lax.optimization_barrier(jnp.sum(share.astype(jnp.float32), axis=1)).reshape(TOKENS, D)
    grad_x = (masked.astype(jnp.float32) + summed).astype(jnp.bfloat16)
    picked_r = picked.astype(jnp.float32).reshape(REPLICAS, MB, FBT, BLK)
    grad_r = grad_pre.astype(jnp.float32).reshape(REPLICAS, MB, FBT, BLK)
    act_r = act.astype(jnp.float32).reshape(REPLICAS, MB, FBT, BLK)
    back_r = back.astype(jnp.float32).reshape(REPLICAS, MB, FBT, BLK)
    part_in = jnp.einsum('rtjc,rtjd->rjcd', picked_r, grad_r).astype(jnp.bfloat16)
    part_out = jnp.einsum('rtjc,rtjd->rjcd', act_r, back_r).astype(jnp.bfloat16)
    grad_in = lax.optimization_barrier(jnp.sum(part_in.astype(jnp.float32), axis=0))
    grad_out = lax.optimization_barrier(jnp.sum(part_out.astype(jnp.float32), axis=0))
    return (grad_x, grad_in, grad_out)

def reference(section_in, out_grad, lengths, w_in, w_out, idx_in, idx_out):
    positions = jnp.arange(MB, dtype=jnp.int32)
    live = (positions[None, None, None, :] < lengths[:, :, :, None]).reshape(2, SECTIONS, TOKENS)
    masked = jnp.where(live[:, :, :, None], out_grad, jnp.zeros((), out_grad.dtype))
    results = []
    for pipe in range(2):
        results.append(lax.map(section_pass, (section_in[pipe], masked[pipe], w_in[:, pipe], w_out[:, pipe], idx_in[:, pipe], idx_out[:, pipe])))
    down_dx, down_in, down_out = results[0]
    up_dx, up_in, up_out = results[1]
    empty = jnp.zeros((1, TOKENS, D), down_dx.dtype)
    from_next = jnp.concatenate([down_dx[1:], empty], axis=0)
    from_prev = jnp.concatenate([empty, up_dx[:-1]], axis=0)
    passed = jnp.stack([from_next, from_prev], axis=0)
    total_in = down_in + jnp.flip(up_in, 0)
    total_out = down_out + jnp.flip(up_out, 0)
    grads = jnp.stack([total_in, total_out], axis=1).reshape(SECTIONS, 2, N_MP, FB_DEV, BLK, BLK)
    return (passed, grads)
```

```python
import functools
import math

import jax
import jax.numpy as jnp
from jax import lax
from jax.experimental import pallas as pl
from jax.experimental.pallas import tpu as pltpu
from jax.sharding import PartitionSpec as P

SCALE = math.sqrt(2.0 / math.pi)
CUBIC = 0.044715


def tick_kernel(relay, per_step, len_ref, idx_in_ref, idx_out_ref, x_ref, g_ref, w_in_ref, w_out_ref,
                keep_in_ref, send_in_ref, keep_out_ref, send_out_ref, share_ref, acc_ref):
    step = pl.program_id(0)
    me = lax.axis_index("dp")
    rows, block = x_ref.shape[0], w_in_ref.shape[-1]
    piece = keep_in_ref.shape[2]
    pieces = block // piece
    live = lax.broadcasted_iota(jnp.int32, (rows, block), 0) < len_ref[relay, 0, 0]

    @pl.when(step == 0)
    def _():
        acc_ref[...] = jnp.zeros_like(acc_ref)

    def put(keep_ref, send_ref, i, value):
        value = value.astype(jnp.bfloat16)
        for q in range(pieces):
            part = value[q * piece:(q + 1) * piece]
            slot = q ^ me

            @pl.when(slot % 2 == 0)
            def _():
                keep_ref[slot // 2, i] = part

            @pl.when(slot % 2 == 1)
            def _():
                send_ref[slot // 2, i] = part

    for i in range(per_step):
        j = step * per_step + i
        from_block = idx_in_ref[0, relay, j]
        to_block = idx_out_ref[0, relay, j]
        picked = x_ref[:, pl.ds(pl.multiple_of(from_block * block, block), block)]
        back = g_ref[:, pl.ds(pl.multiple_of(to_block * block, block), block)]
        back = jnp.where(live, back, jnp.zeros_like(back))
        w_in = w_in_ref[i]
        w_out = w_out_ref[i]
        pre = jnp.dot(picked, w_in, preferred_element_type=jnp.float32)
        back_pre = lax.dot_general(back, w_out, (((1,), (1,)), ((), ())), preferred_element_type=jnp.float32)
        square = pre * pre
        th = jnp.tanh(SCALE * (pre + CUBIC * (square * pre)))
        cdf = 0.5 * (1.0 + th)
        act = (pre * cdf).astype(jnp.bfloat16)
        slope = cdf + (0.5 * pre) * ((1.0 - th) * (1.0 + th)) * (SCALE * (1.0 + (3.0 * CUBIC) * square))
        grad_pre = (back_pre * slope).astype(jnp.bfloat16)
        term = lax.dot_general(grad_pre, w_in, (((1,), (1,)), ((), ())), preferred_element_type=jnp.float32)
        acc_ref[from_block] += term
        over_rows = (((0,), (0,)), ((), ()))
        put(keep_in_ref, send_in_ref, i, lax.dot_general(picked, grad_pre, over_rows, preferred_element_type=jnp.float32))
        put(keep_out_ref, send_out_ref, i, lax.dot_general(act, back, over_rows, preferred_element_type=jnp.float32))

    @pl.when(step == pl.num_programs(0) - 1)
    def _():
        for b in range(acc_ref.shape[0]):
            share_ref[:, b * block:(b + 1) * block] = acc_ref[b].astype(jnp.bfloat16)


def tick(relay, n_dp, lengths, idx_in, idx_out, section_in, out_grad, w_in, w_out):
    rows, width = section_in.shape[2:]
    blocks, block = w_in.shape[2:4]
    per_step = math.gcd(blocks, 8)
    steps = blocks // per_step
    piece = block // n_dp
    whole = pl.BlockSpec((None, None, rows, width), lambda i, *_: (relay, 0, 0, 0))
    weight = pl.BlockSpec((None, None, per_step, block, block), lambda i, *_: (0, relay, i, 0, 0))
    slots = jax.ShapeDtypeStruct((n_dp // 2, blocks, piece, block), jnp.bfloat16)
    slots_spec = pl.BlockSpec((n_dp // 2, per_step, piece, block), lambda i, *_: (0, i, 0, 0))
    return pl.pallas_call(
        functools.partial(tick_kernel, relay, per_step),
        grid_spec=pltpu.PrefetchScalarGridSpec(
            num_scalar_prefetch=3,
            grid=(steps,),
            in_specs=[whole, whole, weight, weight],
            out_specs=[slots_spec] * 4 + [pl.BlockSpec((rows, width), lambda i, *_: (0, 0))],
            scratch_shapes=[pltpu.VMEM((width // block, rows, block), jnp.float32)],
        ),
        out_shape=[slots] * 4 + [jax.ShapeDtypeStruct((rows, width), jnp.bfloat16)],
        compiler_params=pltpu.CompilerParams(
            dimension_semantics=("arbitrary",), vmem_limit_bytes=40 * 1024 * 1024
        ),
        cost_estimate=pl.CostEstimate(
            flops=blocks * 10 * rows * block * block,
            bytes_accessed=blocks * block * block * 8 + rows * width * 6,
            transcendentals=blocks * rows * block,
        ),
        name=f"tick{relay}",
    )(lengths, idx_in, idx_out, section_in, out_grad, w_in, w_out)


def total_kernel(down_in, up_in, down_out, up_out, out):
    out[0] = down_in[...].astype(jnp.float32) + up_in[...].astype(jnp.float32)
    out[1] = down_out[...].astype(jnp.float32) + up_out[...].astype(jnp.float32)


def total_grads(down_in, up_in, down_out, up_out):
    sections, per, piece, block = down_in.shape
    same = pl.BlockSpec((None, per, piece, block), lambda l: (l, 0, 0, 0))
    mirror = pl.BlockSpec((None, per, piece, block), lambda l: (sections - 1 - l, 0, 0, 0))
    return pl.pallas_call(
        total_kernel,
        grid=(sections,),
        in_specs=[same, mirror, same, mirror],
        out_specs=pl.BlockSpec((None, 2, None, per, piece, block), lambda l: (l, 0, 0, 0, 0, 0)),
        out_shape=jax.ShapeDtypeStruct((sections, 2, 1, per, piece, block), jnp.float32),
        name="total",
    )(down_in, up_in, down_out, up_out)


def over_replicas(keep, send, n_dp):
    f32 = jnp.float32
    kept = [keep[k] for k in range(n_dp // 2)]
    got = lax.ppermute(send, "dp", [(d, d ^ 1) for d in range(n_dp)])
    got = [got[k] for k in range(n_dp // 2)]
    sums = [a.astype(f32) + b.astype(f32) for a, b in zip(kept, got)]
    bit = 2
    while bit < n_dp:
        route = [(d, d ^ bit) for d in range(n_dp)]
        odd = jnp.stack([v.astype(jnp.bfloat16) for v in sums[1::2]]) if len(sums) > 2 else sums[1].astype(jnp.bfloat16)
        came = lax.ppermute(odd, "dp", route)
        came = [came[k] for k in range(len(sums) // 2)] if len(sums) > 2 else [came]
        sums = [a + b.astype(f32) for a, b in zip(sums[0::2], came)]
        bit *= 2
    return sums[0].astype(jnp.bfloat16)


def from_behind(value, axis, distance):
    devices = range(lax.axis_size(axis))
    route = [(i - distance, i) for i in devices if i - distance in devices]
    return lax.ppermute(value, axis, route)


def body(section_in, out_grad, lengths, w_in, w_out, idx_in, idx_out):
    n_dp = lax.axis_size("dp")
    n_mp = lax.axis_size("mp")
    sections = lax.axis_size("section")
    rows, width = section_in.shape[2:]
    share_rows = rows // n_mp
    first = lax.axis_index("mp") * share_rows
    moved, passed = [], []
    for relay in range(2):
        keep_in, send_in, keep_out, send_out, share = tick(
            relay, n_dp, lengths, idx_in, idx_out, section_in, out_grad, w_in, w_out
        )
        for keep, send in ((keep_in, send_in), (keep_out, send_out)):
            mine = over_replicas(keep, send, n_dp)
            mine = mine.reshape(sections, -1, *mine.shape[1:])
            moved.append(lax.all_to_all(mine, "section", split_axis=0, concat_axis=0, tiled=True))
        terms = lax.all_to_all(share.reshape(n_mp, share_rows, width), "mp", split_axis=0, concat_axis=0, tiled=True)
        own = lax.dynamic_slice_in_dim(out_grad[relay, 0], first, share_rows, 0)
        live = first + lax.broadcasted_iota(jnp.int32, own.shape, 0) < lengths[relay, 0, 0]
        own = jnp.where(live, own, jnp.zeros_like(own)).astype(jnp.float32)
        dx = (own + jnp.sum(terms.astype(jnp.float32), axis=0)).astype(jnp.bfloat16)
        passed.append(from_behind(dx, "section", 1 if relay else -1))
    grads = total_grads(moved[0], moved[2], moved[1], moved[3])
    return jnp.stack(passed, axis=0)[:, None], grads


def solution(mesh):
    placed = (
        P(None, "section", "dp", None),
        P(None, "section", "dp", None),
        P(None, "section", "dp"),
        P("section", None, "mp", None, None),
        P("section", None, "mp", None, None),
        P("section", None, "mp"),
        P("section", None, "mp"),
    )
    return jax.shard_map(
        body,
        mesh=mesh,
        in_specs=placed,
        out_specs=(
            P(None, "section", ("dp", "mp"), None),
            P(None, None, "mp", "section", "dp", None),
        ),
        check_vma=False,
    )
```

```python
import functools
import math

import jax
import jax.numpy as jnp
from jax import lax
from jax.experimental import pallas as pl
from jax.experimental.pallas import tpu as pltpu
from jax.sharding import PartitionSpec as P

SCALE = math.sqrt(2.0 / math.pi)
CUBIC = 0.044715
GROUP = 4


def tick_kernel(relay, per_step, len_ref, idx_in_ref, idx_out_ref, x_ref, g_ref, w_in_ref, w_out_ref,
                keep_in_ref, send_in_ref, keep_out_ref, send_out_ref, share_ref, acc_ref):
    step = pl.program_id(0)
    me = lax.axis_index("dp")
    rows, block = x_ref.shape[0], w_in_ref.shape[-1]
    piece = keep_in_ref.shape[2]
    pieces = block // piece
    live = lax.broadcasted_iota(jnp.int32, (rows, block), 0) < len_ref[relay, 0, 0]

    @pl.when(step == 0)
    def _():
        acc_ref[...] = jnp.zeros_like(acc_ref)

    odd = me % 2 == 1

    def put(keep_ref, send_ref, i, value):
        value = value.astype(jnp.bfloat16)
        for k in range(pieces // 2):
            low = value[2 * k * piece:(2 * k + 1) * piece]
            high = value[(2 * k + 1) * piece:(2 * k + 2) * piece]
            keep_ref[k ^ (me // 2), i] = jnp.where(odd, high, low)
            send_ref[k ^ (me // 2), i] = jnp.where(odd, low, high)

    f32 = jnp.float32
    over_last = (((1,), (1,)), ((), ()))
    over_rows = (((0,), (0,)), ((), ()))
    for start in range(0, per_step, GROUP):
        group = range(start, min(start + GROUP, per_step))
        sources = [idx_in_ref[0, relay, step * per_step + i] for i in group]
        targets = [idx_out_ref[0, relay, step * per_step + i] for i in group]
        picked = [x_ref[:, pl.ds(pl.multiple_of(b * block, block), block)] for b in sources]
        back = [g_ref[:, pl.ds(pl.multiple_of(b * block, block), block)] for b in targets]
        back = [jnp.where(live, v, jnp.zeros_like(v)) for v in back]
        pre = [jnp.dot(v, w_in_ref[i], preferred_element_type=f32) for v, i in zip(picked, group)]
        back_pre = [lax.dot_general(v, w_out_ref[i], over_last, preferred_element_type=f32) for v, i in zip(back, group)]
        act, grad_pre = [], []
        for v, up in zip(pre, back_pre):
            square = v * v
            th = jnp.tanh(SCALE * (v + CUBIC * (square * v)))
            cdf = 0.5 * (1.0 + th)
            act.append((v * cdf).astype(jnp.bfloat16))
            slope = cdf + (0.5 * v) * ((1.0 - th) * (1.0 + th)) * (SCALE * (1.0 + (3.0 * CUBIC) * square))
            grad_pre.append((up * slope).astype(jnp.bfloat16))
        terms = [lax.dot_general(v, w_in_ref[i], over_last, preferred_element_type=f32) for v, i in zip(grad_pre, group)]
        grad_in = [lax.dot_general(a, v, over_rows, preferred_element_type=f32) for a, v in zip(picked, grad_pre)]
        grad_out = [lax.dot_general(a, v, over_rows, preferred_element_type=f32) for a, v in zip(act, back)]
        for i, b, term, g_in, g_out in zip(group, sources, terms, grad_in, grad_out):
            acc_ref[b] += term
            put(keep_in_ref, send_in_ref, i, g_in)
            put(keep_out_ref, send_out_ref, i, g_out)

    @pl.when(step == pl.num_programs(0) - 1)
    def _():
        for b in range(acc_ref.shape[0]):
            share_ref[:, b * block:(b + 1) * block] = acc_ref[b].astype(jnp.bfloat16)


def tick(relay, n_dp, lengths, idx_in, idx_out, section_in, out_grad, w_in, w_out):
    rows, width = section_in.shape[2:]
    blocks, block = w_in.shape[2:4]
    per_step = math.gcd(blocks, 8)
    steps = blocks // per_step
    piece = block // n_dp
    whole = pl.BlockSpec((None, None, rows, width), lambda i, *_: (relay, 0, 0, 0))
    weight = pl.BlockSpec((None, None, per_step, block, block), lambda i, *_: (0, relay, i, 0, 0))
    slots = jax.ShapeDtypeStruct((n_dp // 2, blocks, piece, block), jnp.bfloat16)
    slots_spec = pl.BlockSpec((n_dp // 2, per_step, piece, block), lambda i, *_: (0, i, 0, 0))
    return pl.pallas_call(
        functools.partial(tick_kernel, relay, per_step),
        grid_spec=pltpu.PrefetchScalarGridSpec(
            num_scalar_prefetch=3,
            grid=(steps,),
            in_specs=[whole, whole, weight, weight],
            out_specs=[slots_spec] * 4 + [pl.BlockSpec((rows, width), lambda i, *_: (0, 0))],
            scratch_shapes=[pltpu.VMEM((width // block, rows, block), jnp.float32)],
        ),
        out_shape=[slots] * 4 + [jax.ShapeDtypeStruct((rows, width), jnp.bfloat16)],
        compiler_params=pltpu.CompilerParams(
            dimension_semantics=("arbitrary",), vmem_limit_bytes=56 * 1024 * 1024
        ),
        cost_estimate=pl.CostEstimate(
            flops=blocks * 10 * rows * block * block,
            bytes_accessed=blocks * block * block * 8 + rows * width * 6,
            transcendentals=blocks * rows * block,
        ),
        name=f"tick{relay}",
    )(lengths, idx_in, idx_out, section_in, out_grad, w_in, w_out)


def total_grads(down_in, up_in, down_out, up_out):
    n = len(down_in)
    me = lax.axis_index("section")

    def by_section(parts):
        stacked = jnp.stack(parts)
        return jnp.stack([lax.dynamic_index_in_dim(stacked, (me - s) % n, 0, keepdims=False) for s in range(n)])

    def both(down, up):
        down, up = by_section(down), by_section(up)
        return down.astype(jnp.float32) + jnp.flip(up, 0).astype(jnp.float32)

    return jnp.stack([both(down_in, up_in), both(down_out, up_out)], axis=1)[:, :, None]


def over_replicas(keep, send, n_dp):
    f32 = jnp.float32
    kept = [keep[k] for k in range(n_dp // 2)]
    got = lax.ppermute(send, "dp", [(d, d ^ 1) for d in range(n_dp)])
    got = [got[k] for k in range(n_dp // 2)]
    sums = [a.astype(f32) + b.astype(f32) for a, b in zip(kept, got)]
    bit = 2
    while bit < n_dp:
        route = [(d, d ^ bit) for d in range(n_dp)]
        odd = jnp.stack([v.astype(jnp.bfloat16) for v in sums[1::2]]) if len(sums) > 2 else sums[1].astype(jnp.bfloat16)
        came = lax.ppermute(odd, "dp", route)
        came = [came[k] for k in range(len(sums) // 2)] if len(sums) > 2 else [came]
        sums = [a + b.astype(f32) for a, b in zip(sums[0::2], came)]
        bit *= 2
    return sums[0].astype(jnp.bfloat16)


def exchange(parts, axis):
    n = lax.axis_size(axis)
    me = lax.axis_index(axis)
    got = []
    for k in range(n):
        part = lax.dynamic_index_in_dim(parts, (me + k) % n, 0, keepdims=False)
        got.append(part if k == 0 else lax.ppermute(part, axis, [(i, (i + k) % n) for i in range(n)]))
    return got


def from_behind(value, axis, distance):
    devices = range(lax.axis_size(axis))
    route = [(i - distance, i) for i in devices if i - distance in devices]
    return lax.ppermute(value, axis, route)


def body(section_in, out_grad, lengths, w_in, w_out, idx_in, idx_out):
    n_dp = lax.axis_size("dp")
    n_mp = lax.axis_size("mp")
    sections = lax.axis_size("section")
    rows, width = section_in.shape[2:]
    share_rows = rows // n_mp
    first = lax.axis_index("mp") * share_rows
    moved, passed = [], []
    for relay in range(2):
        keep_in, send_in, keep_out, send_out, share = tick(
            relay, n_dp, lengths, idx_in, idx_out, section_in, out_grad, w_in, w_out
        )
        for keep, send in ((keep_in, send_in), (keep_out, send_out)):
            mine = over_replicas(keep, send, n_dp)
            mine = mine.reshape(sections, -1, *mine.shape[1:])
            moved.append(exchange(mine, "section"))
        terms = exchange(share.reshape(n_mp, share_rows, width), "mp")
        own = lax.dynamic_slice_in_dim(out_grad[relay, 0], first, share_rows, 0)
        live = first + lax.broadcasted_iota(jnp.int32, own.shape, 0) < lengths[relay, 0, 0]
        own = jnp.where(live, own, jnp.zeros_like(own)).astype(jnp.float32)
        dx = functools.reduce(lambda a, b: a + b.astype(jnp.float32), terms, own).astype(jnp.bfloat16)
        passed.append(from_behind(dx, "section", 1 if relay else -1))
    grads = total_grads(moved[0], moved[2], moved[1], moved[3])
    return jnp.stack(passed, axis=0)[:, None], grads


def solution(mesh):
    placed = (
        P(None, "section", "dp", None),
        P(None, "section", "dp", None),
        P(None, "section", "dp"),
        P("section", None, "mp", None, None),
        P("section", None, "mp", None, None),
        P("section", None, "mp"),
        P("section", None, "mp"),
    )
    return jax.shard_map(
        body,
        mesh=mesh,
        in_specs=placed,
        out_specs=(
            P(None, "section", ("dp", "mp"), None),
            P(None, None, "mp", "section", "dp", None),
        ),
        check_vma=False,
    )
```

```python
import functools
import math

import jax
import jax.numpy as jnp
from jax import lax
from jax.experimental import pallas as pl
from jax.experimental.pallas import tpu as pltpu
from jax.sharding import PartitionSpec as P

SCALE = math.sqrt(2.0 / math.pi)
CUBIC = 0.044715
GROUP = 6
VMEM = 56 * 1024 * 1024
F32 = jnp.float32
BF16 = jnp.bfloat16


def owner(half, turn, sections):
    size = sections // 2
    me = lax.axis_index("section")
    start = jnp.where(half == 1, me, sections - 1 - me)
    base = jnp.where(start < size, 0, size)
    at = start - base + turn
    return base + jnp.where(at < size, at, at - size)


def tick_kernel(relay, first_block, piece_blocks, sections, has_acc, last, n_deps, *refs):
    len_ref, idx_in_ref, idx_out_ref, x_ref, g_ref, w_in_ref, w_out_ref = refs[:7]
    refs = refs[7:]
    if has_acc:
        before_ref, refs = refs[0], refs[1:]
    refs = refs[n_deps:]
    keep_ref, send_ref = refs[:2]
    if last:
        own_ref, other_ref, acc_ref = refs[2:]
    else:
        (acc_ref,) = refs[2:]
    half, turn, part = pl.program_id(0), pl.program_id(1), pl.program_id(2)
    opening = (half == 0) & (turn == 0) & (part == 0)
    closing = (half == 1) & (turn == pl.num_programs(1) - 1) & (part == pl.num_programs(2) - 1)
    me = lax.axis_index("dp")
    per_step, block = w_in_ref.shape[0], w_in_ref.shape[-1]
    rows = x_ref.shape[0]
    piece = keep_ref.shape[3]
    live = lax.broadcasted_iota(jnp.int32, (rows, block), 0) < len_ref[relay, 0, 0]

    @pl.when(opening)
    def _():
        acc_ref[...] = before_ref[...] if has_acc else jnp.zeros_like(acc_ref)

    odd = me % 2 == 1

    def put(kind, i, value):
        value = value.astype(BF16)
        for k in range(block // piece // 2):
            low = value[2 * k * piece:(2 * k + 1) * piece]
            high = value[(2 * k + 1) * piece:(2 * k + 2) * piece]
            keep_ref[k ^ (me // 2), kind, i] = jnp.where(odd, high, low)
            send_ref[k ^ (me // 2), kind, i] = jnp.where(odd, low, high)

    base = owner(half, turn, sections) * piece_blocks + first_block + part * per_step
    over_last = (((1,), (1,)), ((), ()))
    over_rows = (((0,), (0,)), ((), ()))
    for start in range(0, per_step, GROUP):
        group = range(start, min(start + GROUP, per_step))
        sources = [idx_in_ref[0, relay, base + i] for i in group]
        targets = [idx_out_ref[0, relay, base + i] for i in group]
        picked = [x_ref[:, pl.ds(pl.multiple_of(b * block, block), block)] for b in sources]
        back = [g_ref[:, pl.ds(pl.multiple_of(b * block, block), block)] for b in targets]
        back = [jnp.where(live, v, jnp.zeros_like(v)) for v in back]
        pre = [jnp.dot(v, w_in_ref[i], preferred_element_type=F32) for v, i in zip(picked, group)]
        back_pre = [lax.dot_general(v, w_out_ref[i], over_last, preferred_element_type=F32) for v, i in zip(back, group)]
        act, grad_pre = [], []
        for v, up in zip(pre, back_pre):
            square = v * v
            th = jnp.tanh(SCALE * (v + CUBIC * (square * v)))
            cdf = 0.5 * (1.0 + th)
            act.append((v * cdf).astype(BF16))
            slope = cdf + (0.5 * v) * ((1.0 - th) * (1.0 + th)) * (SCALE * (1.0 + (3.0 * CUBIC) * square))
            grad_pre.append((up * slope).astype(BF16))
        terms = [lax.dot_general(v, w_in_ref[i], over_last, preferred_element_type=F32) for v, i in zip(grad_pre, group)]
        grad_in = [lax.dot_general(a, v, over_rows, preferred_element_type=F32) for a, v in zip(picked, grad_pre)]
        grad_out = [lax.dot_general(a, v, over_rows, preferred_element_type=F32) for a, v in zip(act, back)]
        for i, b, term, g_in, g_out in zip(group, sources, terms, grad_in, grad_out):
            acc_ref[b] += term
            put(0, i, g_in)
            put(1, i, g_out)

    if last:
        @pl.when(closing)
        def _():
            at = lax.axis_index("mp")
            share, n_mp = own_ref.shape[0], rows // own_ref.shape[0]
            own_rows = pl.ds(pl.multiple_of(at * share, share), share)
            for b in range(acc_ref.shape[0]):
                columns = slice(b * block, (b + 1) * block)
                held = g_ref[:, columns]
                acc_ref[b] += jnp.where(live & (lax.broadcasted_iota(jnp.int32, (rows, block), 0) // share == at),
                                        held, jnp.zeros_like(held)).astype(F32)
                own_ref[:, columns] = acc_ref[b, own_rows]
                for k in range(1, n_mp):
                    to = lax.rem(at + k, n_mp)
                    there = pl.ds(pl.multiple_of(to * share, share), share)
                    other_ref[k - 1, :, columns] = acc_ref[b, there].astype(BF16)


def tick(relay, lo, hi, before, last, deps, sizes, args):
    sections, n_dp, n_mp = sizes
    lengths, idx_in, idx_out, section_in, out_grad, w_in, w_out = args
    rows, width = section_in.shape[2:]
    blocks, block = w_in.shape[2:4]
    piece_blocks = blocks // sections
    per_step = math.gcd(math.gcd(hi - lo, lo), 6)
    steps = (hi - lo) // per_step
    size = sections // 2
    rows_cut = block // n_dp
    whole = pl.BlockSpec((None, None, rows, width), lambda h, t, i, *_: (relay, 0, 0, 0))
    at_block = lambda h, t, i, *_: (0, relay, (owner(h, t, sections) * piece_blocks + lo) // per_step + i, 0, 0)
    weight = pl.BlockSpec((None, None, per_step, block, block), at_block)
    slots = jax.ShapeDtypeStruct((n_dp // 2, 2, 2, size, hi - lo, rows_cut, block), BF16)
    slots_spec = pl.BlockSpec(
        (n_dp // 2, None, 2, None, per_step, rows_cut, block), lambda h, t, i, *_: (0, h, 0, t, i, 0, 0)
    )
    acc_shape = (width // block, rows, block)
    acc_spec = pl.BlockSpec(acc_shape, lambda h, t, i, *_: (0, 0, 0))
    share = rows // n_mp
    out_specs, out_shape, scratch = [slots_spec] * 2, [slots] * 2, []
    if last:
        out_specs += [
            pl.BlockSpec((share, width), lambda h, t, i, *_: (0, 0)),
            pl.BlockSpec((n_mp - 1, share, width), lambda h, t, i, *_: (0, 0, 0)),
        ]
        out_shape += [jax.ShapeDtypeStruct((share, width), F32), jax.ShapeDtypeStruct((n_mp - 1, share, width), BF16)]
        scratch = [pltpu.VMEM(acc_shape, F32)]
    else:
        out_specs.append(acc_spec)
        out_shape.append(jax.ShapeDtypeStruct(acc_shape, F32))
    held = [] if before is None else [before]
    done = size * 2 * (hi - lo)
    return pl.pallas_call(
        functools.partial(tick_kernel, relay, lo, piece_blocks, sections, bool(held), last, len(deps)),
        grid_spec=pltpu.PrefetchScalarGridSpec(
            num_scalar_prefetch=3,
            grid=(2, size, steps),
            in_specs=[whole, whole, weight, weight] + [acc_spec] * len(held) + [pl.BlockSpec(memory_space=pl.ANY)] * len(deps),
            out_specs=out_specs,
            scratch_shapes=scratch,
        ),
        out_shape=out_shape,
        compiler_params=pltpu.CompilerParams(dimension_semantics=("arbitrary",) * 3, vmem_limit_bytes=VMEM),
        cost_estimate=pl.CostEstimate(
            flops=done * 10 * rows * block * block,
            bytes_accessed=done * block * block * 8 + rows * width * 8,
            transcendentals=done * rows * block,
        ),
        name=f"tick{relay}_{lo}",
    )(lengths, idx_in, idx_out, section_in, out_grad, w_in, w_out, *held, *deps)


def add_kernel(n_terms, apart, n_deps, *refs):
    terms, outs = refs[:n_terms], refs[n_terms + n_deps:]
    for k in range(2):
        total = terms[0][k].astype(F32)
        for term in terms[1:]:
            total += term[k].astype(F32)
        if apart:
            outs[k][...] = total.astype(BF16)
        else:
            outs[0][k] = total.astype(BF16)


def add(terms, apart, name, deps=()):
    shape = terms[0][0].shape[-6:]
    flat = [(a.reshape(-1, math.prod(shape[1:4]), *shape[4:]), k) for a, k in terms]
    count, rows, block = flat[0][0].shape[1:]
    step = math.gcd(count, max(count // 4, 1))
    if apart:
        out_specs = [pl.BlockSpec((step, rows, block), lambda i: (i, 0, 0))] * 2
        out_shape = [jax.ShapeDtypeStruct((count, rows, block), BF16)] * 2
    else:
        out_specs = [pl.BlockSpec((2, step, rows, block), lambda i: (0, i, 0, 0))]
        out_shape = [jax.ShapeDtypeStruct((2, count, rows, block), BF16)]
    outs = pl.pallas_call(
        functools.partial(add_kernel, len(flat), apart, len(deps)),
        grid=(count // step,),
        in_specs=[pl.BlockSpec((2, step, rows, block), lambda i, k=k: (k, i, 0, 0)) for _, k in flat]
        + [pl.BlockSpec(memory_space=pl.ANY)] * len(deps),
        out_specs=out_specs,
        out_shape=out_shape,
        compiler_params=pltpu.CompilerParams(vmem_limit_bytes=VMEM),
        name=name,
    )(*[a for a, _ in flat], *deps)
    return [o.reshape(shape[1:] if apart else shape) for o in outs]


def segments(spans):
    edges = sorted({e for relay in spans for span in relay for e in span})
    found = []
    for a, b in zip(edges, edges[1:]):
        found.append((a - edges[0], b - a, [next((i, a - lo) for i, (lo, hi) in enumerate(relay) if lo <= a < hi) for relay in spans]))
    return found


def mirror_kernel(spans, size, *refs):
    n = [len(relay) for relay in spans]
    own = [refs[:n[0]], refs[n[0]:n[0] + n[1]]]
    far = [refs[sum(n):sum(n) + n[0]], refs[sum(n) + n[0]:2 * sum(n)]]
    outs = refs[2 * sum(n):]
    for start, length, places in segments(spans):
        for r in range(2):
            (i, at), (j, there) = places[r], places[1 - r]
            for turn in range(1, size):
                total = own[r][i][:, turn, at:at + length].astype(F32) + far[1 - r][j][:, turn, there:there + length].astype(F32)
                outs[turn - 1][r, :, start:start + length] = total.astype(BF16)


def mirror_sum(spans, own, far, name):
    _, size, _, rows, block = own[0][0].shape
    long = spans[0][-1][1] - spans[0][0][0]
    flat = own[0] + own[1] + far[0] + far[1]
    return pl.pallas_call(
        functools.partial(mirror_kernel, spans, size),
        out_shape=[jax.ShapeDtypeStruct((2, 2, long, rows, block), BF16)] * (size - 1),
        compiler_params=pltpu.CompilerParams(vmem_limit_bytes=VMEM),
        name=name,
    )(*flat)


def grads_kernel(spans, sections, has_before, *refs):
    size = sections // 2
    n = [len(relay) for relay in spans]
    own = [refs[:n[0]], refs[n[0]:n[0] + n[1]]]
    far = [refs[sum(n):sum(n) + n[0]], refs[sum(n) + n[0]:2 * sum(n)]]
    came = refs[2 * sum(n):2 * sum(n) + size - 1]
    out = refs[-1]
    me = lax.axis_index("section")
    base = jnp.where(me < size, 0, size)
    for start, length, places in segments(spans):
        for r in range(2):
            (i, at), (j, there) = places[r], places[1 - r]
            layer = sections - 1 - me if r else me
            total = own[r][i][:, at:at + length].astype(F32) + far[1 - r][j][:, there:there + length].astype(F32)
            out[layer, :, start:start + length] = total
    for turn in range(1, size):
        at = me - base - turn
        source = base + jnp.where(at < 0, at + size, at)
        for r in range(2):
            out[sections - 1 - source if r else source] = came[turn - 1][r].astype(F32)


def write_grads(spans, own, far, came, before, sections, piece_blocks, name):
    rows, block = own[0][0].shape[3:]
    long = spans[0][-1][1] - spans[0][0][0]
    place = spans[0][0][0] // long
    first = lambda a: pl.BlockSpec((2, None) + a.shape[2:], lambda i: (0, 0, 0, 0, 0))
    flat = own[0] + own[1] + far[0] + far[1]
    held = [] if before is None else [before]
    return pl.pallas_call(
        functools.partial(grads_kernel, spans, sections, bool(held)),
        grid=(1,),
        in_specs=[first(a) for a in flat]
        + [pl.BlockSpec(a.shape, lambda i: (0, 0, 0, 0, 0)) for a in came]
        + [pl.BlockSpec(memory_space=pl.ANY)] * len(held),
        out_specs=pl.BlockSpec((sections, 2, None, long, rows, block), lambda i: (0, 0, 0, place, 0, 0)),
        out_shape=jax.ShapeDtypeStruct((sections, 2, 1, piece_blocks, rows, block), F32),
        input_output_aliases={len(flat) + len(came): 0} if held else {},
        compiler_params=pltpu.CompilerParams(vmem_limit_bytes=VMEM),
        name=name,
    )(*flat, *came, *held)


def from_behind(value, axis, distance):
    devices = range(lax.axis_size(axis))
    route = [(i - distance, i) for i in devices if i - distance in devices]
    return lax.ppermute(value, axis, route)


def flip_bit(value, axis, bit):
    return lax.ppermute(value, axis, [(i, i ^ bit) for i in range(lax.axis_size(axis))])


def turn_half(value, turn):
    size = lax.axis_size("section") // 2
    route = [(h * size + i, h * size + (i + turn) % size) for h in range(2) for i in range(size)]
    return lax.ppermute(value, "section", route)


def body(section_in, out_grad, lengths, w_in, w_out, idx_in, idx_out):
    sections, n_dp, n_mp = (lax.axis_size(a) for a in ("section", "dp", "mp"))
    size = sections // 2
    piece_blocks = w_in.shape[2] // sections
    args = (lengths, idx_in, idx_out, section_in, out_grad, w_in, w_out)
    cuts = [0, piece_blocks // 2, piece_blocks] if piece_blocks % 4 == 0 else [0, piece_blocks]
    fine = sorted(set([0, piece_blocks // 4] + cuts)) if piece_blocks % 4 == 0 else cuts
    chunks = [(0, lo, hi) for lo, hi in zip(fine, fine[1:])] + [(1, lo, hi) for lo, hi in zip(cuts, cuts[1:])]
    mirror = [(i, sections - 1 - i) for i in range(sections)]

    keep, got, sum_a, came, kept, arrived, passed = {}, {}, {}, {}, {}, {}, []
    acc = None

    def stage_a(c):
        deps = [kept[c - 2]] if c - 2 in kept else []
        (sum_a[c],) = add([(keep[c], 1), (got[c], 1)], False, f"core{c}", deps)
        came[c] = flip_bit(sum_a[c], "dp", 2)

    def stage_b(c):
        away, kept[c] = add([(keep[c], 0), (got[c], 0), (came[c], 0)], True, f"pair{c}")
        arrived[c] = lax.ppermute(away, "section", mirror)

    for c, (relay, lo, hi) in enumerate(chunks):
        last = hi == piece_blocks
        deps = [sum_a[c - 2]] if c >= 2 else []
        if c >= 3:
            deps.append(kept[c - 3])
        results = tick(relay, lo, hi, acc, last, deps, (sections, n_dp, n_mp), args)
        keep[c], send = results[:2]
        got[c] = flip_bit(send, "dp", 1)
        acc = None if last else results[2]
        if last:
            dx, others = results[2:]
            for k in range(1, n_mp):
                dx = dx + lax.ppermute(others[k - 1], "mp", [(i, (i + k) % n_mp) for i in range(n_mp)]).astype(F32)
            passed.append(from_behind(dx.astype(BF16), "section", 1 if relay else -1))
        if c >= 1:
            stage_a(c - 1)
        if c >= 2:
            stage_b(c - 2)
    n = len(chunks)
    if n >= 2:
        stage_b(n - 2)
    stage_a(n - 1)
    stage_b(n - 1)

    grads = None
    for lo, hi in zip(cuts, cuts[1:]):
        inside = [[c for c, (r, a, b) in enumerate(chunks) if r == relay and lo <= a < hi] for relay in range(2)]
        spans = [[chunks[c][1:] for c in relay] for relay in inside]
        own = [[kept[c] for c in relay] for relay in inside]
        far = [[arrived[c] for c in relay] for relay in inside]
        to_turn = mirror_sum(spans, own, far, f"mirror_{lo}") if size > 1 else []
        turned = [turn_half(v, turn + 1) for turn, v in enumerate(to_turn)]
        grads = write_grads(spans, own, far, turned, grads, sections, piece_blocks, f"grads_{lo}")
    return jnp.stack(passed, axis=0)[:, None], grads


def solution(mesh):
    placed = (
        P(None, "section", "dp", None),
        P(None, "section", "dp", None),
        P(None, "section", "dp"),
        P("section", None, "mp", None, None),
        P("section", None, "mp", None, None),
        P("section", None, "mp"),
        P("section", None, "mp"),
    )
    return jax.shard_map(
        body,
        mesh=mesh,
        in_specs=placed,
        out_specs=(
            P(None, "section", ("dp", "mp"), None),
            P(None, None, "mp", "section", "dp", None),
        ),
        check_vma=False,
    )
```

```python
import functools
import math

import jax
import jax.numpy as jnp
from jax import lax
from jax.experimental import pallas as pl
from jax.experimental.pallas import tpu as pltpu
from jax.sharding import PartitionSpec as P

SCALE = math.sqrt(2.0 / math.pi)
CUBIC = 0.044715
GROUP = 6
VMEM = 56 * 1024 * 1024
SMALL = pl.CostEstimate(flops=1000, bytes_accessed=1000, transcendentals=0)
F32 = jnp.float32
BF16 = jnp.bfloat16


def owner(half, turn, sections):
    size = sections // 2
    me = lax.axis_index("section")
    start = jnp.where(half == 1, me, sections - 1 - me)
    base = jnp.where(start < size, 0, size)
    at = start - base + turn
    return base + jnp.where(at < size, at, at - size)


def tick_kernel(relay, first_block, piece_blocks, sections, before, last, n_deps, *refs):
    len_ref, idx_in_ref, idx_out_ref, x_ref, g_ref, w_in_ref, w_out_ref = refs[:7]
    before_refs = refs[7:7 + len(before)]
    refs = refs[7 + len(before) + n_deps:]
    keep_ref, send_ref = refs[:2]
    if last:
        own_ref, other_ref, acc_ref = refs[2:]
    else:
        (terms_ref,) = refs[2:]
    half, turn, part = pl.program_id(0), pl.program_id(1), pl.program_id(2)
    opening = (half == 0) & (turn == 0) & (part == 0)
    closing = (half == 1) & (turn == pl.num_programs(1) - 1) & (part == pl.num_programs(2) - 1)
    me = lax.axis_index("dp")
    per_step, block = w_in_ref.shape[0], w_in_ref.shape[-1]
    rows = x_ref.shape[0]
    piece = keep_ref.shape[3]
    live = lax.broadcasted_iota(jnp.int32, (rows, block), 0) < len_ref[relay, 0, 0]

    if last:
        @pl.when(opening)
        def _():
            acc_ref[...] = jnp.zeros_like(acc_ref)
            for lo, ref in zip(before, before_refs):
                size, count = ref.shape[1:3]
                for h in range(2):
                    for t in range(size):
                        at = owner(h, t, sections) * piece_blocks + lo
                        for i in range(count):
                            acc_ref[idx_in_ref[0, relay, at + i]] += ref[h, t, i]

    odd = me % 2 == 1

    def put(kind, i, value):
        value = value.astype(BF16)
        for k in range(block // piece // 2):
            low = value[2 * k * piece:(2 * k + 1) * piece]
            high = value[(2 * k + 1) * piece:(2 * k + 2) * piece]
            keep_ref[k ^ (me // 2), kind, i] = jnp.where(odd, high, low)
            send_ref[k ^ (me // 2), kind, i] = jnp.where(odd, low, high)

    base = owner(half, turn, sections) * piece_blocks + first_block + part * per_step
    over_last = (((1,), (1,)), ((), ()))
    over_rows = (((0,), (0,)), ((), ()))
    for start in range(0, per_step, GROUP):
        group = range(start, min(start + GROUP, per_step))
        sources = [idx_in_ref[0, relay, base + i] for i in group]
        targets = [idx_out_ref[0, relay, base + i] for i in group]
        picked = [x_ref[:, pl.ds(pl.multiple_of(b * block, block), block)] for b in sources]
        back = [g_ref[:, pl.ds(pl.multiple_of(b * block, block), block)] for b in targets]
        back = [jnp.where(live, v, jnp.zeros_like(v)) for v in back]
        pre = [jnp.dot(v, w_in_ref[i], preferred_element_type=F32) for v, i in zip(picked, group)]
        back_pre = [lax.dot_general(v, w_out_ref[i], over_last, preferred_element_type=F32) for v, i in zip(back, group)]
        act, grad_pre = [], []
        for v, up in zip(pre, back_pre):
            square = v * v
            th = jnp.tanh(SCALE * (v + CUBIC * (square * v)))
            cdf = 0.5 * (1.0 + th)
            act.append((v * cdf).astype(BF16))
            slope = cdf + (0.5 * v) * ((1.0 - th) * (1.0 + th)) * (SCALE * (1.0 + (3.0 * CUBIC) * square))
            grad_pre.append((up * slope).astype(BF16))
        terms = [lax.dot_general(v, w_in_ref[i], over_last, preferred_element_type=F32) for v, i in zip(grad_pre, group)]
        grad_in = [lax.dot_general(a, v, over_rows, preferred_element_type=F32) for a, v in zip(picked, grad_pre)]
        grad_out = [lax.dot_general(a, v, over_rows, preferred_element_type=F32) for a, v in zip(act, back)]
        for i, b, term, g_in, g_out in zip(group, sources, terms, grad_in, grad_out):
            if last:
                acc_ref[b] += term
            else:
                terms_ref[i] = term
            put(0, i, g_in)
            put(1, i, g_out)

    if last:
        @pl.when(closing)
        def _():
            at = lax.axis_index("mp")
            share, n_mp = own_ref.shape[0], rows // own_ref.shape[0]
            own_rows = pl.ds(pl.multiple_of(at * share, share), share)
            for b in range(acc_ref.shape[0]):
                columns = slice(b * block, (b + 1) * block)
                held = g_ref[:, columns]
                acc_ref[b] += jnp.where(live & (lax.broadcasted_iota(jnp.int32, (rows, block), 0) // share == at),
                                        held, jnp.zeros_like(held)).astype(F32)
                own_ref[:, columns] = acc_ref[b, own_rows]
                for k in range(1, n_mp):
                    to = lax.rem(at + k, n_mp)
                    there = pl.ds(pl.multiple_of(to * share, share), share)
                    other_ref[k - 1, :, columns] = acc_ref[b, there].astype(BF16)


def tick(relay, lo, hi, before, last, deps, sizes, args):
    sections, n_dp, n_mp = sizes
    lengths, idx_in, idx_out, section_in, out_grad, w_in, w_out = args
    rows, width = section_in.shape[2:]
    blocks, block = w_in.shape[2:4]
    piece_blocks = blocks // sections
    per_step = math.gcd(math.gcd(hi - lo, lo), 6)
    steps = (hi - lo) // per_step
    size = sections // 2
    rows_cut = block // n_dp
    whole = pl.BlockSpec((None, None, rows, width), lambda h, t, i, *_: (relay, 0, 0, 0))
    at_block = lambda h, t, i, *_: (0, relay, (owner(h, t, sections) * piece_blocks + lo) // per_step + i, 0, 0)
    weight = pl.BlockSpec((None, None, per_step, block, block), at_block)
    slots = jax.ShapeDtypeStruct((n_dp // 2, 2, 2, size, hi - lo, rows_cut, block), BF16)
    slots_spec = pl.BlockSpec(
        (n_dp // 2, None, 2, None, per_step, rows_cut, block), lambda h, t, i, *_: (0, h, 0, t, i, 0, 0)
    )
    acc_shape = (width // block, rows, block)
    share = rows // n_mp
    out_specs, out_shape, scratch = [slots_spec] * 2, [slots] * 2, []
    if last:
        out_specs += [
            pl.BlockSpec((share, width), lambda h, t, i, *_: (0, 0)),
            pl.BlockSpec((n_mp - 1, share, width), lambda h, t, i, *_: (0, 0, 0)),
        ]
        out_shape += [jax.ShapeDtypeStruct((share, width), F32), jax.ShapeDtypeStruct((n_mp - 1, share, width), BF16)]
        scratch = [pltpu.VMEM(acc_shape, F32)]
    else:
        out_specs.append(pl.BlockSpec((None, None, per_step, rows, block), lambda h, t, i, *_: (h, t, i, 0, 0)))
        out_shape.append(jax.ShapeDtypeStruct((2, size, hi - lo, rows, block), F32))
    held = [a for _, a in before]
    held_specs = [pl.BlockSpec(a.shape, lambda h, t, i, *_: (0,) * 5) for a in held]
    return pl.pallas_call(
        functools.partial(tick_kernel, relay, lo, piece_blocks, sections, [at for at, _ in before], last, len(deps)),
        grid_spec=pltpu.PrefetchScalarGridSpec(
            num_scalar_prefetch=3,
            grid=(2, size, steps),
            in_specs=[whole, whole, weight, weight] + held_specs + [pl.BlockSpec(memory_space=pl.ANY)] * len(deps),
            out_specs=out_specs,
            scratch_shapes=scratch,
        ),
        out_shape=out_shape,
        compiler_params=pltpu.CompilerParams(dimension_semantics=("arbitrary",) * 3, vmem_limit_bytes=VMEM),
        cost_estimate=SMALL,
        name=f"tick{relay}_{lo}",
    )(lengths, idx_in, idx_out, section_in, out_grad, w_in, w_out, *held, *deps)


def segments(spans):
    edges = sorted({e for relay in spans for span in relay for e in span})
    found = []
    for a, b in zip(edges, edges[1:]):
        found.append((a - edges[0], b - a, [next((i, a - lo) for i, (lo, hi) in enumerate(relay) if lo <= a < hi) for relay in spans]))
    return found


def layer_parts(spans, refs):
    own, far = [], []
    for relay in spans:
        own.append([refs[4 * i:4 * i + 3] for i in range(len(relay))])
        far.append([refs[4 * i + 3] for i in range(len(relay))])
        refs = refs[4 * len(relay):]

    def at(start, length, places, r, index):
        (i, here), (j, there) = places[r], places[1 - r]
        parts = [ref[(slice(None),) + index + (slice(here, here + length),)] for ref in own[r][i]]
        parts.append(far[1 - r][j][(slice(None),) + index + (slice(there, there + length),)])
        return functools.reduce(lambda a, b: a + b, [p.astype(F32) for p in parts])

    return at, refs


def mirror_kernel(spans, size, *refs):
    at, outs = layer_parts(spans, refs)
    for start, length, places in segments(spans):
        for r in range(2):
            for turn in range(1, size):
                outs[turn - 1][r, :, start:start + length] = at(start, length, places, r, (turn,)).astype(BF16)


def cut_operands(groups, turn):
    arrays, specs = [], []
    for relay in groups:
        for keep, got, came, far in relay:
            tail = keep.shape[4:]
            turns = None if turn is not None else keep.shape[3]
            for a, lead in ((keep, (0, 1)), (got, (0, 1)), (came, (1,)), (far, ())):
                arrays.append(a)
                index = lead + (0, turn or 0, 0, 0, 0)
                specs.append(pl.BlockSpec((None,) * len(lead) + (2, turns) + tail, lambda i, index=index: index))
    return arrays, specs


def mirror_sum(spans, groups, name):
    arrays, specs = cut_operands(groups, None)
    size, _, rows, block = arrays[3].shape[1:]
    long = spans[0][-1][1] - spans[0][0][0]
    shape = (2, 2, long, rows, block)
    return pl.pallas_call(
        functools.partial(mirror_kernel, spans, size),
        grid=(1,),
        in_specs=specs,
        out_specs=[pl.BlockSpec(shape, lambda i: (0,) * 5)] * (size - 1),
        out_shape=[jax.ShapeDtypeStruct(shape, BF16)] * (size - 1),
        compiler_params=pltpu.CompilerParams(vmem_limit_bytes=VMEM),
        cost_estimate=SMALL,
        name=name,
    )(*arrays)


def grads_kernel(spans, sections, *refs):
    size = sections // 2
    at, refs = layer_parts(spans, refs)
    came, out = refs[:size - 1], refs[-1]
    me = lax.axis_index("section")
    base = jnp.where(me < size, 0, size)
    for start, length, places in segments(spans):
        for r in range(2):
            out[sections - 1 - me if r else me, :, start:start + length] = at(start, length, places, r, ())
    for turn in range(1, size):
        place = me - base - turn
        source = base + jnp.where(place < 0, place + size, place)
        for r in range(2):
            out[sections - 1 - source if r else source] = came[turn - 1][r].astype(F32)


def write_grads(spans, groups, came, before, sections, piece_blocks, name):
    arrays, specs = cut_operands(groups, 0)
    rows, block = arrays[3].shape[3:]
    long = spans[0][-1][1] - spans[0][0][0]
    place = spans[0][0][0] // long
    held = [] if before is None else [before]
    return pl.pallas_call(
        functools.partial(grads_kernel, spans, sections),
        grid=(1,),
        in_specs=specs
        + [pl.BlockSpec(a.shape, lambda i: (0,) * 5) for a in came]
        + [pl.BlockSpec(memory_space=pl.ANY)] * len(held),
        out_specs=pl.BlockSpec((sections, 2, None, long, rows, block), lambda i: (0, 0, 0, place, 0, 0)),
        out_shape=jax.ShapeDtypeStruct((sections, 2, 1, piece_blocks, rows, block), F32),
        input_output_aliases={len(arrays) + len(came): 0} if held else {},
        compiler_params=pltpu.CompilerParams(vmem_limit_bytes=VMEM),
        cost_estimate=SMALL,
        name=name,
    )(*arrays, *came, *held)


def from_behind(value, axis, distance):
    devices = range(lax.axis_size(axis))
    route = [(i - distance, i) for i in devices if i - distance in devices]
    return lax.ppermute(value, axis, route)


def flip_bit(value, axis, bit):
    return lax.ppermute(value, axis, [(i, i ^ bit) for i in range(lax.axis_size(axis))])


def turn_half(value, turn):
    size = lax.axis_size("section") // 2
    route = [(h * size + i, h * size + (i + turn) % size) for h in range(2) for i in range(size)]
    return lax.ppermute(value, "section", route)


def body(section_in, out_grad, lengths, w_in, w_out, idx_in, idx_out):
    sections, n_dp, n_mp = (lax.axis_size(a) for a in ("section", "dp", "mp"))
    size = sections // 2
    piece_blocks = w_in.shape[2] // sections
    args = (lengths, idx_in, idx_out, section_in, out_grad, w_in, w_out)
    cuts = [0, piece_blocks // 2, piece_blocks] if piece_blocks % 4 == 0 else [0, piece_blocks]
    fine = sorted(set([0, piece_blocks // 4] + cuts)) if piece_blocks % 4 == 0 else cuts
    chunks = [(0, lo, hi) for lo, hi in zip(fine, fine[1:])] + [(1, lo, hi) for lo, hi in zip(cuts, cuts[1:])]
    mirror = [(i, sections - 1 - i) for i in range(sections)]

    keep, got, sum_a, came, away, arrived, passed = {}, {}, {}, {}, {}, {}, []
    before = []

    def stage_a(c):
        sum_a[c] = (keep[c][1].astype(F32) + got[c][1].astype(F32)).astype(BF16)
        came[c] = flip_bit(sum_a[c], "dp", 2)

    def stage_b(c):
        away[c] = (keep[c][0, 0].astype(F32) + got[c][0, 0].astype(F32) + came[c][0].astype(F32)).astype(BF16)
        arrived[c] = lax.ppermute(away[c], "section", mirror)

    for c, (relay, lo, hi) in enumerate(chunks):
        last = hi == piece_blocks
        deps = [sum_a[c - 2]] if c >= 2 else []
        if c >= 3:
            deps.append(away[c - 3])
        results = tick(relay, lo, hi, before, last, deps, (sections, n_dp, n_mp), args)
        keep[c], send = results[:2]
        got[c] = flip_bit(send, "dp", 1)
        before = [] if last else before + [(lo, results[2])]
        if last:
            dx, others = results[2:]
            for k in range(1, n_mp):
                dx = dx + lax.ppermute(others[k - 1], "mp", [(i, (i + k) % n_mp) for i in range(n_mp)]).astype(F32)
            passed.append(from_behind(dx.astype(BF16), "section", 1 if relay else -1))
        if c >= 1:
            stage_a(c - 1)
        if c >= 2:
            stage_b(c - 2)
    n = len(chunks)
    if n >= 2:
        stage_b(n - 2)
    stage_a(n - 1)
    stage_b(n - 1)

    grads = None
    for lo, hi in zip(cuts, cuts[1:]):
        inside = [[c for c, (r, a, b) in enumerate(chunks) if r == relay and lo <= a < hi] for relay in range(2)]
        spans = [[chunks[c][1:] for c in relay] for relay in inside]
        groups = [[(keep[c], got[c], came[c], arrived[c]) for c in relay] for relay in inside]
        to_turn = mirror_sum(spans, groups, f"mirror_{lo}") if size > 1 else []
        turned = [turn_half(v, turn + 1) for turn, v in enumerate(to_turn)]
        grads = write_grads(spans, groups, turned, grads, sections, piece_blocks, f"grads_{lo}")
    return jnp.stack(passed, axis=0)[:, None], grads


def solution(mesh):
    placed = (
        P(None, "section", "dp", None),
        P(None, "section", "dp", None),
        P(None, "section", "dp"),
        P("section", None, "mp", None, None),
        P("section", None, "mp", None, None),
        P("section", None, "mp"),
        P("section", None, "mp"),
    )
    return jax.shard_map(
        body,
        mesh=mesh,
        in_specs=placed,
        out_specs=(
            P(None, "section", ("dp", "mp"), None),
            P(None, None, "mp", "section", "dp", None),
        ),
        check_vma=False,
    )
```

```python
import functools
import math

import jax
import jax.numpy as jnp
from jax import lax
from jax.experimental import pallas as pl
from jax.experimental.pallas import tpu as pltpu
from jax.sharding import PartitionSpec as P

SCALE = math.sqrt(2.0 / math.pi)
CUBIC = 0.044715
GROUP = 6
DEPTH = 2
VMEM = 56 * 1024 * 1024
SMALL = pl.CostEstimate(flops=1000, bytes_accessed=1000, transcendentals=0)
LARGE = pl.CostEstimate(flops=1000, bytes_accessed=2 * 10**8, transcendentals=0)
F32 = jnp.float32
BF16 = jnp.bfloat16


def owner(half, turn, sections):
    size = sections // 2
    me = lax.axis_index("section")
    start = jnp.where(half == 1, me, sections - 1 - me)
    base = jnp.where(start < size, 0, size)
    at = start - base + turn
    return base + jnp.where(at < size, at, at - size)


def tick_kernel(relay, first_block, piece_blocks, sections, n_mp, before, last, n_deps, *refs):
    len_ref, idx_in_ref, idx_out_ref, x_ref, g_ref, w_in_ref, w_out_ref = refs[:7]
    before_refs = refs[7:7 + len(before)]
    refs = refs[7 + len(before) + n_deps:]
    keep_ref, send_ref = refs[:2]
    if last:
        share_ref, acc_ref = refs[2:]
    else:
        (terms_ref,) = refs[2:]
    half, turn, part = pl.program_id(0), pl.program_id(1), pl.program_id(2)
    opening = (half == 0) & (turn == 0) & (part == 0)
    closing = (half == 1) & (turn == pl.num_programs(1) - 1) & (part == pl.num_programs(2) - 1)
    me = lax.axis_index("dp")
    per_step, block = w_in_ref.shape[0], w_in_ref.shape[-1]
    rows = x_ref.shape[0]
    piece = keep_ref.shape[3]
    live = lax.broadcasted_iota(jnp.int32, (rows, block), 0) < len_ref[relay]

    if last:
        @pl.when(opening)
        def _():
            acc_ref[...] = jnp.zeros_like(acc_ref)
            for lo, ref in zip(before, before_refs):
                size, count = ref.shape[1:3]
                for h in range(2):
                    for t in range(size):
                        at = owner(h, t, sections) * piece_blocks + lo
                        for i in range(count):
                            acc_ref[idx_in_ref[0, relay, at + i]] += ref[h, t, i]

    odd = me % 2 == 1

    def put(kind, i, value):
        value = value.astype(BF16)
        for k in range(block // piece // 2):
            low = value[2 * k * piece:(2 * k + 1) * piece]
            high = value[(2 * k + 1) * piece:(2 * k + 2) * piece]
            keep_ref[k ^ (me // 2), kind, i] = jnp.where(odd, high, low)
            send_ref[k ^ (me // 2), kind, i] = jnp.where(odd, low, high)

    base = owner(half, turn, sections) * piece_blocks + first_block + part * per_step
    over_last = (((1,), (1,)), ((), ()))
    over_rows = (((0,), (0,)), ((), ()))
    for start in range(0, per_step, GROUP):
        group = range(start, min(start + GROUP, per_step))
        sources = [idx_in_ref[0, relay, base + i] for i in group]
        targets = [idx_out_ref[0, relay, base + i] for i in group]
        picked = [x_ref[:, pl.ds(pl.multiple_of(b * block, block), block)] for b in sources]
        back = [g_ref[:, pl.ds(pl.multiple_of(b * block, block), block)] for b in targets]
        back = [jnp.where(live, v, jnp.zeros_like(v)) for v in back]
        pre = [jnp.dot(v, w_in_ref[i], preferred_element_type=F32) for v, i in zip(picked, group)]
        back_pre = [lax.dot_general(v, w_out_ref[i], over_last, preferred_element_type=F32) for v, i in zip(back, group)]
        act, grad_pre = [], []
        for v, up in zip(pre, back_pre):
            square = v * v
            th = jnp.tanh(SCALE * (v + CUBIC * (square * v)))
            cdf = 0.5 * (1.0 + th)
            act.append((v * cdf).astype(BF16))
            slope = cdf + (0.5 * v) * ((1.0 - th) * (1.0 + th)) * (SCALE * (1.0 + (3.0 * CUBIC) * square))
            grad_pre.append((up * slope).astype(BF16))
        terms = [lax.dot_general(v, w_in_ref[i], over_last, preferred_element_type=F32) for v, i in zip(grad_pre, group)]
        grad_in = [lax.dot_general(a, v, over_rows, preferred_element_type=F32) for a, v in zip(picked, grad_pre)]
        grad_out = [lax.dot_general(a, v, over_rows, preferred_element_type=F32) for a, v in zip(act, back)]
        for i, b, term, g_in, g_out in zip(group, sources, terms, grad_in, grad_out):
            if last:
                acc_ref[b] += term
            else:
                terms_ref[i] = term
            put(0, i, g_in)
            put(1, i, g_out)

    if last:
        @pl.when(closing)
        def _():
            share = rows // n_mp
            owned = lax.broadcasted_iota(jnp.int32, (rows, block), 0) // share == lax.axis_index("mp")
            for b in range(acc_ref.shape[0]):
                columns = slice(b * block, (b + 1) * block)
                held = g_ref[:, columns]
                held = jnp.where(live & owned, held, jnp.zeros_like(held)).astype(F32)
                share_ref[:, columns] = (acc_ref[b] + held).astype(BF16)


def tick(relay, lo, hi, before, last, deps, sizes, args):
    sections, n_dp, n_mp = sizes
    lengths, idx_in, idx_out, section_in, out_grad, w_in, w_out = args
    rows, width = section_in.shape[2:]
    blocks, block = w_in.shape[2:4]
    piece_blocks = blocks // sections
    per_step = math.gcd(math.gcd(hi - lo, lo), 6)
    steps = (hi - lo) // per_step
    size = sections // 2
    rows_cut = block // n_dp
    whole = pl.BlockSpec((None, None, rows, width), lambda h, t, i, *_: (relay, 0, 0, 0))
    at_block = lambda h, t, i, *_: (0, relay, (owner(h, t, sections) * piece_blocks + lo) // per_step + i, 0, 0)
    weight = pl.BlockSpec((None, None, per_step, block, block), at_block)
    slots = jax.ShapeDtypeStruct((n_dp // 2, 2, 2, size, hi - lo, rows_cut, block), BF16)
    slots_spec = pl.BlockSpec(
        (n_dp // 2, None, 2, None, per_step, rows_cut, block), lambda h, t, i, *_: (0, h, 0, t, i, 0, 0)
    )
    acc_shape = (width // block, rows, block)
    out_specs, out_shape, scratch = [slots_spec] * 2, [slots] * 2, []
    if last:
        out_specs.append(pl.BlockSpec((rows, width), lambda h, t, i, *_: (0, 0)))
        out_shape.append(jax.ShapeDtypeStruct((rows, width), BF16))
        scratch = [pltpu.VMEM(acc_shape, F32)]
    else:
        out_specs.append(pl.BlockSpec((None, None, per_step, rows, block), lambda h, t, i, *_: (h, t, i, 0, 0)))
        out_shape.append(jax.ShapeDtypeStruct((2, size, hi - lo, rows, block), F32))
    held = [a for _, a in before]
    held_specs = [pl.BlockSpec(a.shape, lambda h, t, i, *_: (0,) * 5) for a in held]
    return pl.pallas_call(
        functools.partial(tick_kernel, relay, lo, piece_blocks, sections, n_mp, [at for at, _ in before], last, len(deps)),
        grid_spec=pltpu.PrefetchScalarGridSpec(
            num_scalar_prefetch=3,
            grid=(2, size, steps),
            in_specs=[whole, whole, weight, weight] + held_specs + [pl.BlockSpec(memory_space=pl.ANY)] * len(deps),
            out_specs=out_specs,
            scratch_shapes=scratch,
        ),
        out_shape=out_shape,
        compiler_params=pltpu.CompilerParams(dimension_semantics=("arbitrary",) * 3, vmem_limit_bytes=VMEM),
        cost_estimate=LARGE,
        name=f"tick{relay}_{lo}",
    )(lengths, idx_in, idx_out, section_in, out_grad, w_in, w_out, *held, *deps)


def segments(spans):
    edges = sorted({e for relay in spans for span in relay for e in span})
    found = []
    for a, b in zip(edges, edges[1:]):
        found.append((a - edges[0], b - a, [next((i, a - lo) for i, (lo, hi) in enumerate(relay) if lo <= a < hi) for relay in spans]))
    return found


def layer_parts(spans, refs):
    own, far = [], []
    for relay in spans:
        own.append([refs[4 * i:4 * i + 3] for i in range(len(relay))])
        far.append([refs[4 * i + 3] for i in range(len(relay))])
        refs = refs[4 * len(relay):]

    def at(start, length, places, r, index):
        (i, here), (j, there) = places[r], places[1 - r]
        parts = [ref[(slice(None),) + index + (slice(here, here + length),)] for ref in own[r][i]]
        parts.append(far[1 - r][j][(slice(None),) + index + (slice(there, there + length),)])
        return functools.reduce(lambda a, b: a + b, [p.astype(F32) for p in parts])

    return at, refs


def mirror_kernel(spans, size, *refs):
    at, outs = layer_parts(spans, refs)
    for start, length, places in segments(spans):
        for r in range(2):
            for turn in range(1, size):
                outs[turn - 1][r, :, start:start + length] = at(start, length, places, r, (turn,)).astype(BF16)


def cut_operands(groups, turn):
    arrays, specs = [], []
    for relay in groups:
        for keep, got, came, far in relay:
            tail = keep.shape[4:]
            turns = None if turn is not None else keep.shape[3]
            for a, lead in ((keep, (0, 1)), (got, (0, 1)), (came, (1,)), (far, ())):
                arrays.append(a)
                index = lead + (0, turn or 0, 0, 0, 0)
                specs.append(pl.BlockSpec((None,) * len(lead) + (2, turns) + tail, lambda i, index=index: index))
    return arrays, specs


def mirror_sum(spans, groups, name):
    arrays, specs = cut_operands(groups, None)
    size, _, rows, block = arrays[3].shape[1:]
    long = spans[0][-1][1] - spans[0][0][0]
    shape = (2, 2, long, rows, block)
    return pl.pallas_call(
        functools.partial(mirror_kernel, spans, size),
        grid=(1,),
        in_specs=specs,
        out_specs=[pl.BlockSpec(shape, lambda i: (0,) * 5)] * (size - 1),
        out_shape=[jax.ShapeDtypeStruct(shape, BF16)] * (size - 1),
        compiler_params=pltpu.CompilerParams(vmem_limit_bytes=VMEM),
        cost_estimate=SMALL,
        name=name,
    )(*arrays)


def grads_kernel(spans, sections, *refs):
    size = sections // 2
    at, refs = layer_parts(spans, refs)
    came, out = refs[:size - 1], refs[-1]
    me = lax.axis_index("section")
    base = jnp.where(me < size, 0, size)
    for start, length, places in segments(spans):
        for r in range(2):
            out[sections - 1 - me if r else me, :, start:start + length] = at(start, length, places, r, ())
    for turn in range(1, size):
        place = me - base - turn
        source = base + jnp.where(place < 0, place + size, place)
        for r in range(2):
            out[sections - 1 - source if r else source] = came[turn - 1][r].astype(F32)


def write_grads(spans, groups, came, before, sections, piece_blocks, name):
    arrays, specs = cut_operands(groups, 0)
    rows, block = arrays[3].shape[3:]
    long = spans[0][-1][1] - spans[0][0][0]
    place = spans[0][0][0] // long
    held = [] if before is None else [before]
    return pl.pallas_call(
        functools.partial(grads_kernel, spans, sections),
        grid=(1,),
        in_specs=specs
        + [pl.BlockSpec(a.shape, lambda i: (0,) * 5) for a in came]
        + [pl.BlockSpec(memory_space=pl.ANY)] * len(held),
        out_specs=pl.BlockSpec((sections, 2, None, long, rows, block), lambda i: (0, 0, 0, place, 0, 0)),
        out_shape=jax.ShapeDtypeStruct((sections, 2, 1, piece_blocks, rows, block), F32),
        input_output_aliases={len(arrays) + len(came): 0} if held else {},
        compiler_params=pltpu.CompilerParams(vmem_limit_bytes=VMEM),
        cost_estimate=SMALL,
        name=name,
    )(*arrays, *came, *held)


def tie(value, *deps):
    any_space = pl.BlockSpec(memory_space=pl.ANY)
    return pl.pallas_call(
        lambda *refs: None,
        in_specs=[any_space] * (1 + len(deps)),
        out_specs=any_space,
        out_shape=jax.ShapeDtypeStruct(value.shape, value.dtype),
        input_output_aliases={0: 0},
        cost_estimate=SMALL,
        name="tie",
    )(value, *deps)


def from_behind(value, axis, distance):
    devices = range(lax.axis_size(axis))
    route = [(i - distance, i) for i in devices if i - distance in devices]
    return lax.ppermute(value, axis, route)


def flip_bit(value, axis, bit):
    return lax.ppermute(value, axis, [(i, i ^ bit) for i in range(lax.axis_size(axis))])


def turn_half(value, turn):
    size = lax.axis_size("section") // 2
    route = [(h * size + i, h * size + (i + turn) % size) for h in range(2) for i in range(size)]
    return lax.ppermute(value, "section", route)


def body(section_in, out_grad, lengths, w_in, w_out, idx_in, idx_out):
    sections, n_dp, n_mp = (lax.axis_size(a) for a in ("section", "dp", "mp"))
    size = sections // 2
    piece_blocks = w_in.shape[2] // sections
    args = (lengths.reshape(2), idx_in, idx_out, section_in, out_grad, w_in, w_out)
    cuts = [0, piece_blocks // 2, piece_blocks] if piece_blocks % 4 == 0 else [0, piece_blocks]
    fine = sorted(set([0, piece_blocks // 4] + cuts)) if piece_blocks % 4 == 0 else cuts
    chunks = [(0, lo, hi) for lo, hi in zip(fine, fine[1:])] + [(1, lo, hi) for lo, hi in zip(cuts, cuts[1:])]
    mirror = [(i, sections - 1 - i) for i in range(sections)]

    keep, got, sum_a, came, away, arrived, dx, passed = {}, {}, {}, {}, {}, {}, {}, {}
    before, shares = [], []
    x_queue, z_queue = [], []

    def queued(queue, operand, move):
        if len(queue) >= DEPTH:
            operand = tie(operand, queue[-DEPTH])
        queue.append(move(operand))
        return queue[-1]

    def stage_a(c):
        sum_a[c] = (keep[c][1].astype(F32) + got[c][1].astype(F32)).astype(BF16)
        came[c] = queued(x_queue, sum_a[c], lambda v: flip_bit(v, "dp", 2))

    def stage_b(c):
        away[c] = (keep[c][0, 0].astype(F32) + got[c][0, 0].astype(F32) + came[c][0].astype(F32)).astype(BF16)
        arrived[c] = queued(z_queue, away[c], lambda v: lax.ppermute(v, "section", mirror))
        for relay in (r for r in range(2) if dx_after[r] == c):
            passed[relay] = queued(z_queue, dx[relay], lambda v: from_behind(v, "section", 1 if relay else -1))

    ends = [max(c for c, chunk in enumerate(chunks) if chunk[0] == r) for r in range(2)]
    dx_after = [2, 3] if len(chunks) > 4 else ends
    for c, (relay, lo, hi) in enumerate(chunks):
        last = hi == piece_blocks
        if c == 2:
            stage_a(1)
        deps = [sum_a[c - 2]] if c >= 2 else []
        if c == 2:
            deps.append(sum_a[1])
        if c >= 3:
            deps.append(away[c - 3])
        if c >= 4:
            deps.append(arrived[c - 4])
        results = tick(relay, lo, hi, before, last, deps, (sections, n_dp, n_mp), args)
        keep[c], send = results[:2]
        got[c] = flip_bit(send, "dp", 1)
        before = [] if last else before + [(lo, results[2])]
        if last:
            shares.append((relay, results[2]))
        if c + 1 == len(chunks):
            for r, share in shares:
                if r != relay:
                    share = tie(share, keep[c])
                dx[r] = lax.psum_scatter(share, "mp", scatter_dimension=0, tiled=True)
        if c >= 1 and c != 2:
            stage_a(c - 1)
        if c >= 2:
            stage_b(c - 2)
    n = len(chunks)
    if n >= 2:
        stage_b(n - 2)
    stage_a(n - 1)
    stage_b(n - 1)

    grads = None
    for lo, hi in zip(cuts, cuts[1:]):
        inside = [[c for c, (r, a, b) in enumerate(chunks) if r == relay and lo <= a < hi] for relay in range(2)]
        spans = [[chunks[c][1:] for c in relay] for relay in inside]
        groups = [[(keep[c], got[c], came[c], arrived[c]) for c in relay] for relay in inside]
        to_turn = mirror_sum(spans, groups, f"mirror_{lo}") if size > 1 else []
        turned = [queued(z_queue, v, lambda v, turn=turn: turn_half(v, turn + 1)) for turn, v in enumerate(to_turn)]
        grads = write_grads(spans, groups, turned, grads, sections, piece_blocks, f"grads_{lo}")
    return jnp.stack([passed[0], passed[1]], axis=0)[:, None], grads


def solution(mesh):
    placed = (
        P(None, "section", "dp", None),
        P(None, "section", "dp", None),
        P(None, "section", "dp"),
        P("section", None, "mp", None, None),
        P("section", None, "mp", None, None),
        P("section", None, "mp"),
        P("section", None, "mp"),
    )
    return jax.shard_map(
        body,
        mesh=mesh,
        in_specs=placed,
        out_specs=(
            P(None, "section", ("dp", "mp"), None),
            P(None, None, "mp", "section", "dp", None),
        ),
        check_vma=False,
    )
```

```python
import functools
import math

import jax
import jax.numpy as jnp
from jax import lax
from jax.experimental import pallas as pl
from jax.experimental.pallas import tpu as pltpu
from jax.sharding import PartitionSpec as P

SCALE = math.sqrt(2.0 / math.pi)
CUBIC = 0.044715
GROUP = 4
STEP = 8


def tick_kernel(relay, per_step, n_deps, len_ref, idx_in_ref, idx_out_ref, x_ref, g_ref, w_in_ref, w_out_ref, *refs):
    keep_ref, send_ref, own_ref, other_ref, acc_ref = refs[n_deps:]
    step = pl.program_id(0)
    me = lax.axis_index("dp")
    rows, block = x_ref.shape[0], w_in_ref.shape[-1]
    piece = keep_ref.shape[3]
    pieces = block // piece
    live = lax.broadcasted_iota(jnp.int32, (rows, block), 0) < len_ref[relay]

    @pl.when(step == 0)
    def _():
        acc_ref[...] = jnp.zeros_like(acc_ref)

    odd = me % 2 == 1

    def put(kind, i, value):
        value = value.astype(jnp.bfloat16)
        for k in range(pieces // 2):
            low = value[2 * k * piece:(2 * k + 1) * piece]
            high = value[(2 * k + 1) * piece:(2 * k + 2) * piece]
            keep_ref[k ^ (me // 2), kind, i] = jnp.where(odd, high, low)
            send_ref[k ^ (me // 2), kind, i] = jnp.where(odd, low, high)

    f32 = jnp.float32
    over_last = (((1,), (1,)), ((), ()))
    over_rows = (((0,), (0,)), ((), ()))
    for start in range(0, per_step, GROUP):
        group = range(start, min(start + GROUP, per_step))
        sources = [idx_in_ref[0, relay, step * per_step + i] for i in group]
        targets = [idx_out_ref[0, relay, step * per_step + i] for i in group]
        picked = [x_ref[:, pl.ds(pl.multiple_of(b * block, block), block)] for b in sources]
        back = [g_ref[:, pl.ds(pl.multiple_of(b * block, block), block)] for b in targets]
        back = [jnp.where(live, v, jnp.zeros_like(v)) for v in back]
        pre = [jnp.dot(v, w_in_ref[i], preferred_element_type=f32) for v, i in zip(picked, group)]
        back_pre = [lax.dot_general(v, w_out_ref[i], over_last, preferred_element_type=f32) for v, i in zip(back, group)]
        act, grad_pre = [], []
        for v, up in zip(pre, back_pre):
            square = v * v
            th = jnp.tanh(SCALE * (v + CUBIC * (square * v)))
            cdf = 0.5 * (1.0 + th)
            act.append((v * cdf).astype(jnp.bfloat16))
            slope = cdf + (0.5 * v) * ((1.0 - th) * (1.0 + th)) * (SCALE * (1.0 + (3.0 * CUBIC) * square))
            grad_pre.append((up * slope).astype(jnp.bfloat16))
        terms = [lax.dot_general(v, w_in_ref[i], over_last, preferred_element_type=f32) for v, i in zip(grad_pre, group)]
        grad_in = [lax.dot_general(a, v, over_rows, preferred_element_type=f32) for a, v in zip(picked, grad_pre)]
        grad_out = [lax.dot_general(a, v, over_rows, preferred_element_type=f32) for a, v in zip(act, back)]
        for i, b, term, g_in, g_out in zip(group, sources, terms, grad_in, grad_out):
            acc_ref[b] += term
            put(0, i, g_in)
            put(1, i, g_out)

    @pl.when(step == pl.num_programs(0) - 1)
    def _():
        at = lax.axis_index("mp")
        share, n_mp = own_ref.shape[0], rows // own_ref.shape[0]
        owned = live & (lax.broadcasted_iota(jnp.int32, (rows, block), 0) // share == at)
        for b in range(acc_ref.shape[0]):
            columns = slice(b * block, (b + 1) * block)
            held = g_ref[:, columns]
            acc_ref[b] += jnp.where(owned, held, jnp.zeros_like(held)).astype(jnp.float32)
            own_ref[:, columns] = acc_ref[b, pl.ds(pl.multiple_of(at * share, share), share)]
            for k in range(1, n_mp):
                there = pl.multiple_of(lax.rem(at + k, n_mp) * share, share)
                other_ref[k - 1, :, columns] = acc_ref[b, pl.ds(there, share)].astype(jnp.bfloat16)


def tick(relay, sizes, deps, lengths, idx_in, idx_out, section_in, out_grad, w_in, w_out):
    sections, n_dp, n_mp = sizes
    rows, width = section_in.shape[2:]
    blocks, block = w_in.shape[2:4]
    per = blocks // sections
    per_step = math.gcd(per, STEP)
    turns = per // per_step
    piece, share = block // n_dp, rows // n_mp
    whole = pl.BlockSpec((None, None, rows, width), lambda i, *_: (relay, 0, 0, 0))
    weight = pl.BlockSpec((None, None, per_step, block, block), lambda i, *_: (0, relay, i, 0, 0))
    slots = jax.ShapeDtypeStruct((n_dp // 2, sections, 2, per, piece, block), jnp.bfloat16)
    slots_spec = pl.BlockSpec(
        (n_dp // 2, None, 2, per_step, piece, block), lambda i, *_: (0, i // turns, 0, i % turns, 0, 0)
    )
    return pl.pallas_call(
        functools.partial(tick_kernel, relay, per_step, len(deps)),
        grid_spec=pltpu.PrefetchScalarGridSpec(
            num_scalar_prefetch=3,
            grid=(sections * turns,),
            in_specs=[whole, whole, weight, weight] + [pl.BlockSpec(memory_space=pl.ANY)] * len(deps),
            out_specs=[slots_spec] * 2
            + [pl.BlockSpec((share, width), lambda i, *_: (0, 0)), pl.BlockSpec((n_mp - 1, share, width), lambda i, *_: (0, 0, 0))],
            scratch_shapes=[pltpu.VMEM((width // block, rows, block), jnp.float32)],
        ),
        out_shape=[slots] * 2
        + [jax.ShapeDtypeStruct((share, width), jnp.float32), jax.ShapeDtypeStruct((n_mp - 1, share, width), jnp.bfloat16)],
        compiler_params=pltpu.CompilerParams(
            dimension_semantics=("arbitrary",), vmem_limit_bytes=56 * 1024 * 1024
        ),
        cost_estimate=pl.CostEstimate(
            flops=blocks * 10 * rows * block * block,
            bytes_accessed=blocks * block * block * 8 + rows * width * 6,
            transcendentals=blocks * rows * block,
        ),
        name=f"tick{relay}",
    )(lengths, idx_in, idx_out, section_in, out_grad, w_in, w_out, *deps)


def total(*parts):
    return functools.reduce(lambda a, b: a + b, [p.astype(jnp.float32) for p in parts])


def tie(value, *deps):
    any_space = pl.BlockSpec(memory_space=pl.ANY)
    return pl.pallas_call(
        lambda *refs: None,
        in_specs=[any_space] * (1 + len(deps)),
        out_specs=any_space,
        out_shape=jax.ShapeDtypeStruct(value.shape, value.dtype),
        input_output_aliases={0: 0},
        cost_estimate=pl.CostEstimate(flops=1000, bytes_accessed=1000, transcendentals=0),
        name="tie",
    )(value, *deps)


def flip_bit(value, axis, bit):
    return lax.ppermute(value, axis, [(i, i ^ bit) for i in range(lax.axis_size(axis))])


def from_behind(value, axis, distance):
    devices = range(lax.axis_size(axis))
    route = [(i - distance, i) for i in devices if i - distance in devices]
    return lax.ppermute(value, axis, route)


def body(section_in, out_grad, lengths, w_in, w_out, idx_in, idx_out):
    sections, n_dp, n_mp = sizes = tuple(lax.axis_size(a) for a in ("section", "dp", "mp"))
    per = w_in.shape[2] // sections
    args = (lengths.reshape(2), idx_in, idx_out, section_in, out_grad, w_in, w_out)
    keep, got, own, others = [], [], [], []
    for relay in range(2):
        kept, send, mine, theirs = tick(relay, sizes, keep, *args)
        keep.append(kept)
        got.append(flip_bit(send, "dp", 1))
        own.append(mine)
        others.append([lax.ppermute(theirs[k - 1], "mp", [(i, (i + k) % n_mp) for i in range(n_mp)]) for k in range(1, n_mp)])
    small = per // 3 if per % 3 == 0 else per
    cuts = [(0, small), (small, per)] if small < per else [(0, per)]
    chunks = [(relay, cut) for cut in cuts for relay in range(2)]

    def parts(slot, relay, cut):
        return [v[relay][slot][:, :, cut[0]:cut[1]] for v in (keep, got)]

    sums = [total(*parts(1, *chunk)).astype(jnp.bfloat16) for chunk in chunks]
    came = [flip_bit(tie(v, *sums[:i]) if i > 1 else v, "dp", 2) for i, v in enumerate(sums)]
    passed = []
    for relay in range(2):
        dx = total(tie(own[relay], *sums), *others[relay]).astype(jnp.bfloat16)
        passed.append(from_behind(dx, "section", 1 if relay else -1))
    moved = {}
    for chunk, far in zip(chunks, came):
        mine = total(*parts(0, *chunk), far).astype(jnp.bfloat16)
        moved[chunk] = lax.all_to_all(mine, "section", split_axis=0, concat_axis=0, tiled=True)
    grads = jnp.concatenate([total(moved[0, cut], jnp.flip(moved[1, cut], 0)) for cut in cuts], axis=2)
    return jnp.stack(passed, axis=0)[:, None], grads[:, :, None]


def solution(mesh):
    placed = (
        P(None, "section", "dp", None),
        P(None, "section", "dp", None),
        P(None, "section", "dp"),
        P("section", None, "mp", None, None),
        P("section", None, "mp", None, None),
        P("section", None, "mp"),
        P("section", None, "mp"),
    )
    return jax.shard_map(
        body,
        mesh=mesh,
        in_specs=placed,
        out_specs=(
            P(None, "section", ("dp", "mp"), None),
            P(None, None, "mp", "section", "dp", None),
        ),
        check_vma=False,
    )
```

```python
import functools
import math

import jax
import jax.numpy as jnp
from jax import lax
from jax.experimental import pallas as pl
from jax.experimental.pallas import tpu as pltpu
from jax.sharding import PartitionSpec as P

SCALE = math.sqrt(2.0 / math.pi)
CUBIC = 0.044715
GROUP = 4


def tick_kernel(relay, per_step, n_mp, n_deps, len_ref, idx_in_ref, idx_out_ref, x_ref, g_ref, w_in_ref, w_out_ref, *refs):
    keep_in_ref, send_in_ref, keep_out_ref, send_out_ref, share_ref, acc_ref = refs[n_deps:]
    step = pl.program_id(0)
    me = lax.axis_index("dp")
    rows, block = x_ref.shape[0], w_in_ref.shape[-1]
    piece = keep_in_ref.shape[2]
    pieces = block // piece
    live = lax.broadcasted_iota(jnp.int32, (rows, block), 0) < len_ref[relay]

    @pl.when(step == 0)
    def _():
        acc_ref[...] = jnp.zeros_like(acc_ref)

    odd = me % 2 == 1

    def put(keep_ref, send_ref, i, value):
        value = value.astype(jnp.bfloat16)
        for k in range(pieces // 2):
            low = value[2 * k * piece:(2 * k + 1) * piece]
            high = value[(2 * k + 1) * piece:(2 * k + 2) * piece]
            keep_ref[k ^ (me // 2), i] = jnp.where(odd, high, low)
            send_ref[k ^ (me // 2), i] = jnp.where(odd, low, high)

    f32 = jnp.float32
    over_last = (((1,), (1,)), ((), ()))
    over_rows = (((0,), (0,)), ((), ()))
    for start in range(0, per_step, GROUP):
        group = range(start, min(start + GROUP, per_step))
        sources = [idx_in_ref[0, relay, step * per_step + i] for i in group]
        targets = [idx_out_ref[0, relay, step * per_step + i] for i in group]
        picked = [x_ref[:, pl.ds(pl.multiple_of(b * block, block), block)] for b in sources]
        back = [g_ref[:, pl.ds(pl.multiple_of(b * block, block), block)] for b in targets]
        back = [jnp.where(live, v, jnp.zeros_like(v)) for v in back]
        pre = [jnp.dot(v, w_in_ref[i], preferred_element_type=f32) for v, i in zip(picked, group)]
        back_pre = [lax.dot_general(v, w_out_ref[i], over_last, preferred_element_type=f32) for v, i in zip(back, group)]
        act, grad_pre = [], []
        for v, up in zip(pre, back_pre):
            square = v * v
            th = jnp.tanh(SCALE * (v + CUBIC * (square * v)))
            cdf = 0.5 * (1.0 + th)
            act.append((v * cdf).astype(jnp.bfloat16))
            slope = cdf + (0.5 * v) * ((1.0 - th) * (1.0 + th)) * (SCALE * (1.0 + (3.0 * CUBIC) * square))
            grad_pre.append((up * slope).astype(jnp.bfloat16))
        terms = [lax.dot_general(v, w_in_ref[i], over_last, preferred_element_type=f32) for v, i in zip(grad_pre, group)]
        grad_in = [lax.dot_general(a, v, over_rows, preferred_element_type=f32) for a, v in zip(picked, grad_pre)]
        grad_out = [lax.dot_general(a, v, over_rows, preferred_element_type=f32) for a, v in zip(act, back)]
        for i, b, term, g_in, g_out in zip(group, sources, terms, grad_in, grad_out):
            acc_ref[b] += term
            put(keep_in_ref, send_in_ref, i, g_in)
            put(keep_out_ref, send_out_ref, i, g_out)

    @pl.when(step == pl.num_programs(0) - 1)
    def _():
        share = rows // n_mp
        owned = live & (lax.broadcasted_iota(jnp.int32, (rows, block), 0) // share == lax.axis_index("mp"))
        for b in range(acc_ref.shape[0]):
            columns = slice(b * block, (b + 1) * block)
            held = g_ref[:, columns]
            held = jnp.where(owned, held, jnp.zeros_like(held)).astype(jnp.float32)
            share_ref[:, columns] = (acc_ref[b] + held).astype(jnp.bfloat16)


def tick(relay, n_dp, n_mp, deps, lengths, idx_in, idx_out, section_in, out_grad, w_in, w_out):
    rows, width = section_in.shape[2:]
    blocks, block = w_in.shape[2:4]
    per_step = math.gcd(blocks, 8)
    steps = blocks // per_step
    piece = block // n_dp
    whole = pl.BlockSpec((None, None, rows, width), lambda i, *_: (relay, 0, 0, 0))
    weight = pl.BlockSpec((None, None, per_step, block, block), lambda i, *_: (0, relay, i, 0, 0))
    slots = jax.ShapeDtypeStruct((n_dp // 2, blocks, piece, block), jnp.bfloat16)
    slots_spec = pl.BlockSpec((n_dp // 2, per_step, piece, block), lambda i, *_: (0, i, 0, 0))
    return pl.pallas_call(
        functools.partial(tick_kernel, relay, per_step, n_mp, len(deps)),
        grid_spec=pltpu.PrefetchScalarGridSpec(
            num_scalar_prefetch=3,
            grid=(steps,),
            in_specs=[whole, whole, weight, weight] + [pl.BlockSpec(memory_space=pl.ANY)] * len(deps),
            out_specs=[slots_spec] * 4 + [pl.BlockSpec((rows, width), lambda i, *_: (0, 0))],
            scratch_shapes=[pltpu.VMEM((width // block, rows, block), jnp.float32)],
        ),
        out_shape=[slots] * 4 + [jax.ShapeDtypeStruct((rows, width), jnp.bfloat16)],
        compiler_params=pltpu.CompilerParams(
            dimension_semantics=("arbitrary",), vmem_limit_bytes=56 * 1024 * 1024
        ),
        cost_estimate=pl.CostEstimate(
            flops=blocks * 10 * rows * block * block,
            bytes_accessed=blocks * block * block * 8 + rows * width * 6,
            transcendentals=blocks * rows * block,
        ),
        name=f"tick{relay}",
    )(lengths, idx_in, idx_out, section_in, out_grad, w_in, w_out, *deps)


def total(*parts):
    return functools.reduce(lambda a, b: a + b, [p.astype(jnp.float32) for p in parts])


def tie(value, *deps):
    any_space = pl.BlockSpec(memory_space=pl.ANY)
    return pl.pallas_call(
        lambda *refs: None,
        in_specs=[any_space] * (1 + len(deps)),
        out_specs=any_space,
        out_shape=jax.ShapeDtypeStruct(value.shape, value.dtype),
        input_output_aliases={0: 0},
        cost_estimate=pl.CostEstimate(flops=1000, bytes_accessed=1000, transcendentals=0),
        name="tie",
    )(value, *deps)


def flip_bit(value, axis, bit):
    return lax.ppermute(value, axis, [(i, i ^ bit) for i in range(lax.axis_size(axis))])


def from_behind(value, axis, distance):
    devices = range(lax.axis_size(axis))
    route = [(i - distance, i) for i in devices if i - distance in devices]
    return lax.ppermute(value, axis, route)


def body(section_in, out_grad, lengths, w_in, w_out, idx_in, idx_out):
    sections, n_dp, n_mp = (lax.axis_size(a) for a in ("section", "dp", "mp"))
    args = (lengths.reshape(2), idx_in, idx_out, section_in, out_grad, w_in, w_out)
    keep, got, dx = [], [], []
    for relay in range(2):
        keep_in, send_in, keep_out, send_out, share = tick(relay, n_dp, n_mp, keep[:1], *args)
        keep += [keep_in, keep_out]
        got += [flip_bit(send_in, "dp", 1), flip_bit(send_out, "dp", 1)]
        dx.append(lax.psum_scatter(share, "mp", scatter_dimension=0, tiled=True))
    sums = [total(k[1], g[1]).astype(jnp.bfloat16) for k, g in zip(keep, got)]
    came = [flip_bit(tie(v, *sums[:i]) if i else v, "dp", 2) for i, v in enumerate(sums)]
    passed = [from_behind(v, "section", distance) for v, distance in zip(dx, (-1, 1))]
    moved = []
    for i, (k, g, far) in enumerate(zip(keep, got, came)):
        mine = total(k[0], g[0], tie(far, *(sums if i == 0 else [mine]))).astype(jnp.bfloat16)
        mine = mine.reshape(sections, -1, *mine.shape[1:])
        moved.append(lax.all_to_all(mine, "section", split_axis=0, concat_axis=0, tiled=True))
    grads = jnp.stack([total(moved[i], jnp.flip(moved[i + 2], 0)) for i in range(2)], axis=1)
    return jnp.stack(passed, axis=0)[:, None], grads[:, :, None]


def solution(mesh):
    placed = (
        P(None, "section", "dp", None),
        P(None, "section", "dp", None),
        P(None, "section", "dp"),
        P("section", None, "mp", None, None),
        P("section", None, "mp", None, None),
        P("section", None, "mp"),
        P("section", None, "mp"),
    )
    return jax.shard_map(
        body,
        mesh=mesh,
        in_specs=placed,
        out_specs=(
            P(None, "section", ("dp", "mp"), None),
            P(None, None, "mp", "section", "dp", None),
        ),
        check_vma=False,
    )
```

```python
import functools
import math

import jax
import jax.numpy as jnp
from jax import lax
from jax.experimental import pallas as pl
from jax.experimental.pallas import tpu as pltpu
from jax.sharding import PartitionSpec as P

SCALE = math.sqrt(2.0 / math.pi)
CUBIC = 0.044715
GROUP = 4


def tick_kernel(relay, per_step, n_deps, len_ref, idx_in_ref, idx_out_ref, x_ref, g_ref, w_in_ref, w_out_ref, *refs):
    grad_in_ref, grad_out_ref, own_ref, other_ref, acc_ref = refs[n_deps:]
    step = pl.program_id(0)
    rows, block = x_ref.shape[0], w_in_ref.shape[-1]
    piece = grad_in_ref.shape[2]
    pieces = block // piece
    live = lax.broadcasted_iota(jnp.int32, (rows, block), 0) < len_ref[relay]

    @pl.when(step == 0)
    def _():
        acc_ref[...] = jnp.zeros_like(acc_ref)

    def put(ref, i, value):
        value = value.astype(jnp.bfloat16)
        for q in range(pieces):
            ref[q, i] = value[q * piece:(q + 1) * piece]

    f32 = jnp.float32
    over_last = (((1,), (1,)), ((), ()))
    over_rows = (((0,), (0,)), ((), ()))
    for start in range(0, per_step, GROUP):
        group = range(start, min(start + GROUP, per_step))
        sources = [idx_in_ref[0, relay, step * per_step + i] for i in group]
        targets = [idx_out_ref[0, relay, step * per_step + i] for i in group]
        picked = [x_ref[:, pl.ds(pl.multiple_of(b * block, block), block)] for b in sources]
        back = [g_ref[:, pl.ds(pl.multiple_of(b * block, block), block)] for b in targets]
        back = [jnp.where(live, v, jnp.zeros_like(v)) for v in back]
        pre = [jnp.dot(v, w_in_ref[i], preferred_element_type=f32) for v, i in zip(picked, group)]
        back_pre = [lax.dot_general(v, w_out_ref[i], over_last, preferred_element_type=f32) for v, i in zip(back, group)]
        act, grad_pre = [], []
        for v, up in zip(pre, back_pre):
            square = v * v
            th = jnp.tanh(SCALE * (v + CUBIC * (square * v)))
            cdf = 0.5 * (1.0 + th)
            act.append((v * cdf).astype(jnp.bfloat16))
            slope = cdf + (0.5 * v) * ((1.0 - th) * (1.0 + th)) * (SCALE * (1.0 + (3.0 * CUBIC) * square))
            grad_pre.append((up * slope).astype(jnp.bfloat16))
        terms = [lax.dot_general(v, w_in_ref[i], over_last, preferred_element_type=f32) for v, i in zip(grad_pre, group)]
        grad_in = [lax.dot_general(a, v, over_rows, preferred_element_type=f32) for a, v in zip(picked, grad_pre)]
        grad_out = [lax.dot_general(a, v, over_rows, preferred_element_type=f32) for a, v in zip(act, back)]
        for i, b, term, g_in, g_out in zip(group, sources, terms, grad_in, grad_out):
            acc_ref[b] += term
            put(grad_in_ref, i, g_in)
            put(grad_out_ref, i, g_out)

    @pl.when(step == pl.num_programs(0) - 1)
    def _():
        at = lax.axis_index("mp")
        share, n_mp = own_ref.shape[0], rows // own_ref.shape[0]
        owned = live & (lax.broadcasted_iota(jnp.int32, (rows, block), 0) // share == at)
        for b in range(acc_ref.shape[0]):
            columns = slice(b * block, (b + 1) * block)
            held = g_ref[:, columns]
            acc_ref[b] += jnp.where(owned, held, jnp.zeros_like(held)).astype(jnp.float32)
            own_ref[:, columns] = acc_ref[b, pl.ds(pl.multiple_of(at * share, share), share)]
            for k in range(1, n_mp):
                there = pl.multiple_of(lax.rem(at + k, n_mp) * share, share)
                other_ref[k - 1, :, columns] = acc_ref[b, pl.ds(there, share)].astype(jnp.bfloat16)


def tick(relay, n_dp, n_mp, deps, lengths, idx_in, idx_out, section_in, out_grad, w_in, w_out):
    rows, width = section_in.shape[2:]
    blocks, block = w_in.shape[2:4]
    per_step = math.gcd(blocks, 8)
    steps = blocks // per_step
    piece, share = block // n_dp, rows // n_mp
    whole = pl.BlockSpec((None, None, rows, width), lambda i, *_: (relay, 0, 0, 0))
    weight = pl.BlockSpec((None, None, per_step, block, block), lambda i, *_: (0, relay, i, 0, 0))
    slots = jax.ShapeDtypeStruct((n_dp, blocks, piece, block), jnp.bfloat16)
    slots_spec = pl.BlockSpec((n_dp, per_step, piece, block), lambda i, *_: (0, i, 0, 0))
    return pl.pallas_call(
        functools.partial(tick_kernel, relay, per_step, len(deps)),
        grid_spec=pltpu.PrefetchScalarGridSpec(
            num_scalar_prefetch=3,
            grid=(steps,),
            in_specs=[whole, whole, weight, weight] + [pl.BlockSpec(memory_space=pl.ANY)] * len(deps),
            out_specs=[slots_spec] * 2
            + [pl.BlockSpec((share, width), lambda i, *_: (0, 0)), pl.BlockSpec((n_mp - 1, share, width), lambda i, *_: (0, 0, 0))],
            scratch_shapes=[pltpu.VMEM((width // block, rows, block), jnp.float32)],
        ),
        out_shape=[slots] * 2
        + [jax.ShapeDtypeStruct((share, width), jnp.float32), jax.ShapeDtypeStruct((n_mp - 1, share, width), jnp.bfloat16)],
        compiler_params=pltpu.CompilerParams(
            dimension_semantics=("arbitrary",), vmem_limit_bytes=56 * 1024 * 1024
        ),
        cost_estimate=pl.CostEstimate(
            flops=blocks * 10 * rows * block * block,
            bytes_accessed=blocks * block * block * 8 + rows * width * 6,
            transcendentals=blocks * rows * block,
        ),
        name=f"tick{relay}",
    )(lengths, idx_in, idx_out, section_in, out_grad, w_in, w_out, *deps)


def total(*parts):
    return functools.reduce(lambda a, b: a + b, [p.astype(jnp.float32) for p in parts])


def from_behind(value, axis, distance):
    devices = range(lax.axis_size(axis))
    route = [(i - distance, i) for i in devices if i - distance in devices]
    return lax.ppermute(value, axis, route)


def body(section_in, out_grad, lengths, w_in, w_out, idx_in, idx_out):
    sections, n_dp, n_mp = (lax.axis_size(a) for a in ("section", "dp", "mp"))
    args = (lengths.reshape(2), idx_in, idx_out, section_in, out_grad, w_in, w_out)
    moved, own, others, done = [], [], [], []
    for relay in range(2):
        *partials, mine, theirs = tick(relay, n_dp, n_mp, done, *args)
        done = partials[:1]
        for partial in partials:
            summed = lax.psum_scatter(partial, "dp", scatter_dimension=0, tiled=True)
            summed = summed.reshape(sections, -1, *summed.shape[2:])
            moved.append(lax.all_to_all(summed, "section", split_axis=0, concat_axis=0, tiled=True))
        own.append(mine)
        others.append([lax.ppermute(theirs[k - 1], "mp", [(i, (i + k) % n_mp) for i in range(n_mp)]) for k in range(1, n_mp)])
    passed = []
    for relay in range(2):
        dx = total(own[relay], *others[relay]).astype(jnp.bfloat16)
        passed.append(from_behind(dx, "section", 1 if relay else -1))
    grads = jnp.stack([total(moved[i], jnp.flip(moved[i + 2], 0)) for i in range(2)], axis=1)
    return jnp.stack(passed, axis=0)[:, None], grads[:, :, None]


def solution(mesh):
    placed = (
        P(None, "section", "dp", None),
        P(None, "section", "dp", None),
        P(None, "section", "dp"),
        P("section", None, "mp", None, None),
        P("section", None, "mp", None, None),
        P("section", None, "mp"),
        P("section", None, "mp"),
    )
    return jax.shard_map(
        body,
        mesh=mesh,
        in_specs=placed,
        out_specs=(
            P(None, "section", ("dp", "mp"), None),
            P(None, None, "mp", "section", "dp", None),
        ),
        check_vma=False,
    )
```

```python
import functools
import math

import jax
import jax.numpy as jnp
from jax import lax
from jax.experimental import pallas as pl
from jax.experimental.pallas import tpu as pltpu
from jax.sharding import PartitionSpec as P

SCALE = math.sqrt(2.0 / math.pi)
CUBIC = 0.044715
GROUP = 4


def tick_kernel(relay, per_step, n_mp, n_deps, len_ref, idx_in_ref, idx_out_ref, x_ref, g_ref, w_in_ref, w_out_ref, *refs):
    *slot_refs, share_ref, acc_ref = refs[n_deps:]
    step = pl.program_id(0)
    me = lax.axis_index("dp")
    rows, block = x_ref.shape[0], w_in_ref.shape[-1]
    piece = slot_refs[0].shape[2]
    live = lax.broadcasted_iota(jnp.int32, (rows, block), 0) < len_ref[relay]

    @pl.when(step == 0)
    def _():
        acc_ref[...] = jnp.zeros_like(acc_ref)

    odd, high = me % 2 == 1, me // 2 == 1

    def put(kind, i, value):
        value = value.astype(jnp.bfloat16)
        p = [value[q * piece:(q + 1) * piece] for q in range(4)]
        even = [jnp.where(odd, p[k + 1], p[k]) for k in (0, 2)]
        other = [jnp.where(odd, p[k], p[k + 1]) for k in (0, 2)]
        for slot, pair in ((0, even), (1, other)):
            slot_refs[slot][kind, i] = jnp.where(high, pair[1], pair[0])
            slot_refs[slot + 2][kind, i] = jnp.where(high, pair[0], pair[1])

    f32 = jnp.float32
    over_last = (((1,), (1,)), ((), ()))
    over_rows = (((0,), (0,)), ((), ()))
    for start in range(0, per_step, GROUP):
        group = range(start, min(start + GROUP, per_step))
        sources = [idx_in_ref[0, relay, step * per_step + i] for i in group]
        targets = [idx_out_ref[0, relay, step * per_step + i] for i in group]
        picked = [x_ref[:, pl.ds(pl.multiple_of(b * block, block), block)] for b in sources]
        back = [g_ref[:, pl.ds(pl.multiple_of(b * block, block), block)] for b in targets]
        back = [jnp.where(live, v, jnp.zeros_like(v)) for v in back]
        pre = [jnp.dot(v, w_in_ref[i], preferred_element_type=f32) for v, i in zip(picked, group)]
        back_pre = [lax.dot_general(v, w_out_ref[i], over_last, preferred_element_type=f32) for v, i in zip(back, group)]
        act, grad_pre = [], []
        for v, up in zip(pre, back_pre):
            square = v * v
            th = jnp.tanh(SCALE * (v + CUBIC * (square * v)))
            cdf = 0.5 * (1.0 + th)
            act.append((v * cdf).astype(jnp.bfloat16))
            slope = cdf + (0.5 * v) * ((1.0 - th) * (1.0 + th)) * (SCALE * (1.0 + (3.0 * CUBIC) * square))
            grad_pre.append((up * slope).astype(jnp.bfloat16))
        terms = [lax.dot_general(v, w_in_ref[i], over_last, preferred_element_type=f32) for v, i in zip(grad_pre, group)]
        grad_in = [lax.dot_general(a, v, over_rows, preferred_element_type=f32) for a, v in zip(picked, grad_pre)]
        grad_out = [lax.dot_general(a, v, over_rows, preferred_element_type=f32) for a, v in zip(act, back)]
        for i, b, term, g_in, g_out in zip(group, sources, terms, grad_in, grad_out):
            acc_ref[b] += term
            put(0, i, g_in)
            put(1, i, g_out)

    @pl.when(step == pl.num_programs(0) - 1)
    def _():
        share = rows // n_mp
        owned = live & (lax.broadcasted_iota(jnp.int32, (rows, block), 0) // share == lax.axis_index("mp"))
        for b in range(acc_ref.shape[0]):
            columns = slice(b * block, (b + 1) * block)
            held = g_ref[:, columns]
            held = jnp.where(owned, held, jnp.zeros_like(held)).astype(jnp.float32)
            share_ref[:, columns] = (acc_ref[b] + held).astype(jnp.bfloat16)


def tick(relay, sections, n_dp, n_mp, deps, lengths, idx_in, idx_out, section_in, out_grad, w_in, w_out):
    rows, width = section_in.shape[2:]
    blocks, block = w_in.shape[2:4]
    per = blocks // sections
    per_step = math.gcd(per, 8)
    turns = per // per_step
    piece = block // n_dp
    whole = pl.BlockSpec((None, None, rows, width), lambda i, *_: (relay, 0, 0, 0))
    weight = pl.BlockSpec((None, None, per_step, block, block), lambda i, *_: (0, relay, i, 0, 0))
    slots = jax.ShapeDtypeStruct((sections, 2, per, piece, block), jnp.bfloat16)
    slots_spec = pl.BlockSpec((None, 2, per_step, piece, block), lambda i, *_: (i // turns, 0, i % turns, 0, 0))
    return pl.pallas_call(
        functools.partial(tick_kernel, relay, per_step, n_mp, len(deps)),
        grid_spec=pltpu.PrefetchScalarGridSpec(
            num_scalar_prefetch=3,
            grid=(sections * turns,),
            in_specs=[whole, whole, weight, weight] + [pl.BlockSpec(memory_space=pl.ANY)] * len(deps),
            out_specs=[slots_spec] * 4 + [pl.BlockSpec((rows, width), lambda i, *_: (0, 0))],
            scratch_shapes=[pltpu.VMEM((width // block, rows, block), jnp.float32)],
        ),
        out_shape=[slots] * 4 + [jax.ShapeDtypeStruct((rows, width), jnp.bfloat16)],
        compiler_params=pltpu.CompilerParams(
            dimension_semantics=("arbitrary",), vmem_limit_bytes=56 * 1024 * 1024
        ),
        cost_estimate=pl.CostEstimate(
            flops=blocks * 10 * rows * block * block,
            bytes_accessed=blocks * block * block * 8 + rows * width * 6,
            transcendentals=blocks * rows * block,
        ),
        name=f"tick{relay}",
    )(lengths, idx_in, idx_out, section_in, out_grad, w_in, w_out, *deps)


def total(*parts):
    return functools.reduce(lambda a, b: a + b, [p.astype(jnp.float32) for p in parts])


def tie(value, *deps):
    any_space = pl.BlockSpec(memory_space=pl.ANY)
    return pl.pallas_call(
        lambda *refs: None,
        in_specs=[any_space] * (1 + len(deps)),
        out_specs=any_space,
        out_shape=jax.ShapeDtypeStruct(value.shape, value.dtype),
        input_output_aliases={0: 0},
        cost_estimate=pl.CostEstimate(flops=1000, bytes_accessed=1000, transcendentals=0),
        name="tie",
    )(value, *deps)


def flip_bit(value, axis, bit):
    return lax.ppermute(value, axis, [(i, i ^ bit) for i in range(lax.axis_size(axis))])


def from_behind(value, axis, distance):
    devices = range(lax.axis_size(axis))
    route = [(i - distance, i) for i in devices if i - distance in devices]
    return lax.ppermute(value, axis, route)


def rotate(parts, axis):
    n = lax.axis_size(axis)
    me = lax.axis_index(axis)
    got = []
    for k in range(n):
        part = lax.dynamic_index_in_dim(parts, lax.rem(me + k, n), 0, keepdims=False)
        got.append(part if k == 0 else lax.ppermute(part, axis, [(i, (i + k) % n) for i in range(n)]))
    return got


def by_source(parts, axis):
    n = len(parts)
    me = lax.axis_index(axis)
    stacked = jnp.stack(parts)
    return jnp.stack([lax.dynamic_index_in_dim(stacked, lax.rem(me - k + n, n), 0, keepdims=False) for k in range(n)])


def body(section_in, out_grad, lengths, w_in, w_out, idx_in, idx_out):
    sections, n_dp, n_mp = (lax.axis_size(a) for a in ("section", "dp", "mp"))
    args = (lengths.reshape(2), idx_in, idx_out, section_in, out_grad, w_in, w_out)

    def scatter(share):
        return lax.psum_scatter(share, "mp", scatter_dimension=0, tiled=True)

    a0, s0, a2, s2, share0 = tick(0, sections, n_dp, n_mp, [], *args)
    got0, got2 = flip_bit(s0, "dp", 1), flip_bit(s2, "dp", 1)
    sum0 = total(a2, got2).astype(jnp.bfloat16)
    came0 = flip_bit(sum0, "dp", 2)
    b0, t0, b2, t2, share1 = tick(1, sections, n_dp, n_mp, [sum0], *args)
    hot0, hot2 = flip_bit(t0, "dp", 1), flip_bit(t2, "dp", 1)
    dx0 = scatter(share0)
    sum1 = total(tie(b2, came0), hot2).astype(jnp.bfloat16)
    came1 = flip_bit(sum1, "dp", 2)
    dx1 = scatter(tie(share1, came0))
    moved0 = rotate(total(a0, got0, came0).astype(jnp.bfloat16), "section")
    passed0 = from_behind(dx0, "section", -1)
    passed1 = from_behind(dx1, "section", 1)
    moved1 = rotate(total(b0, hot0, came1).astype(jnp.bfloat16), "section")
    grads = total(by_source(moved0, "section"), jnp.flip(by_source(moved1, "section"), 0))
    return jnp.stack([passed0, passed1], axis=0)[:, None], grads[:, :, None]


def solution(mesh):
    placed = (
        P(None, "section", "dp", None),
        P(None, "section", "dp", None),
        P(None, "section", "dp"),
        P("section", None, "mp", None, None),
        P("section", None, "mp", None, None),
        P("section", None, "mp"),
        P("section", None, "mp"),
    )
    return jax.shard_map(
        body,
        mesh=mesh,
        in_specs=placed,
        out_specs=(
            P(None, "section", ("dp", "mp"), None),
            P(None, None, "mp", "section", "dp", None),
        ),
        check_vma=False,
    )
```

```python
import functools
import math

import jax
import jax.numpy as jnp
from jax import lax
from jax.experimental import pallas as pl
from jax.experimental.pallas import tpu as pltpu
from jax.sharding import PartitionSpec as P

SCALE = math.sqrt(2.0 / math.pi)
CUBIC = 0.044715
GROUP = 4


def tick_kernel(relay, per_step, n_mp, apart, n_deps, len_ref, idx_in_ref, idx_out_ref, x_ref, g_ref, w_in_ref, w_out_ref, *refs):
    *slot_refs, share_ref, acc_ref = refs[n_deps:]
    step = pl.program_id(0)
    me = lax.axis_index("dp")
    rows, block = x_ref.shape[0], w_in_ref.shape[-1]
    piece = slot_refs[0].shape[-2]
    live = lax.broadcasted_iota(jnp.int32, (rows, block), 0) < len_ref[relay]

    @pl.when(step == 0)
    def _():
        acc_ref[...] = jnp.zeros_like(acc_ref)

    odd, high = me % 2 == 1, me // 2 == 1

    def put(kind, i, value):
        value = value.astype(jnp.bfloat16)
        p = [value[q * piece:(q + 1) * piece] for q in range(4)]
        even = [jnp.where(odd, p[k + 1], p[k]) for k in (0, 2)]
        other = [jnp.where(odd, p[k], p[k + 1]) for k in (0, 2)]
        for slot, pair in ((0, even), (1, other)):
            for at, v in ((slot, jnp.where(high, pair[1], pair[0])), (slot + 2, jnp.where(high, pair[0], pair[1]))):
                if apart:
                    slot_refs[2 * at + kind][i] = v
                else:
                    slot_refs[at][kind, i] = v

    f32 = jnp.float32
    over_last = (((1,), (1,)), ((), ()))
    over_rows = (((0,), (0,)), ((), ()))
    for start in range(0, per_step, GROUP):
        group = range(start, min(start + GROUP, per_step))
        sources = [idx_in_ref[0, relay, step * per_step + i] for i in group]
        targets = [idx_out_ref[0, relay, step * per_step + i] for i in group]
        picked = [x_ref[:, pl.ds(pl.multiple_of(b * block, block), block)] for b in sources]
        back = [g_ref[:, pl.ds(pl.multiple_of(b * block, block), block)] for b in targets]
        back = [jnp.where(live, v, jnp.zeros_like(v)) for v in back]
        pre = [jnp.dot(v, w_in_ref[i], preferred_element_type=f32) for v, i in zip(picked, group)]
        back_pre = [lax.dot_general(v, w_out_ref[i], over_last, preferred_element_type=f32) for v, i in zip(back, group)]
        act, grad_pre = [], []
        for v, up in zip(pre, back_pre):
            square = v * v
            th = jnp.tanh(SCALE * (v + CUBIC * (square * v)))
            cdf = 0.5 * (1.0 + th)
            act.append((v * cdf).astype(jnp.bfloat16))
            slope = cdf + (0.5 * v) * ((1.0 - th) * (1.0 + th)) * (SCALE * (1.0 + (3.0 * CUBIC) * square))
            grad_pre.append((up * slope).astype(jnp.bfloat16))
        terms = [lax.dot_general(v, w_in_ref[i], over_last, preferred_element_type=f32) for v, i in zip(grad_pre, group)]
        grad_in = [lax.dot_general(a, v, over_rows, preferred_element_type=f32) for a, v in zip(picked, grad_pre)]
        grad_out = [lax.dot_general(a, v, over_rows, preferred_element_type=f32) for a, v in zip(act, back)]
        for i, b, term, g_in, g_out in zip(group, sources, terms, grad_in, grad_out):
            acc_ref[b] += term
            put(0, i, g_in)
            put(1, i, g_out)

    @pl.when(step == pl.num_programs(0) - 1)
    def _():
        share = rows // n_mp
        owned = live & (lax.broadcasted_iota(jnp.int32, (rows, block), 0) // share == lax.axis_index("mp"))
        for b in range(acc_ref.shape[0]):
            columns = slice(b * block, (b + 1) * block)
            held = g_ref[:, columns]
            held = jnp.where(owned, held, jnp.zeros_like(held)).astype(jnp.float32)
            share_ref[:, columns] = (acc_ref[b] + held).astype(jnp.bfloat16)


def tick(relay, sections, n_dp, n_mp, apart, deps, lengths, idx_in, idx_out, section_in, out_grad, w_in, w_out):
    rows, width = section_in.shape[2:]
    blocks, block = w_in.shape[2:4]
    per = blocks // sections
    per_step = math.gcd(per, 8)
    turns = per // per_step
    piece = block // n_dp
    whole = pl.BlockSpec((None, None, rows, width), lambda i, *_: (relay, 0, 0, 0))
    weight = pl.BlockSpec((None, None, per_step, block, block), lambda i, *_: (0, relay, i, 0, 0))
    if apart:
        slots = [jax.ShapeDtypeStruct((sections, per, piece, block), jnp.bfloat16)] * 8
        slots_spec = [pl.BlockSpec((None, per_step, piece, block), lambda i, *_: (i // turns, i % turns, 0, 0))] * 8
    else:
        slots = [jax.ShapeDtypeStruct((sections, 2, per, piece, block), jnp.bfloat16)] * 4
        slots_spec = [pl.BlockSpec((None, 2, per_step, piece, block), lambda i, *_: (i // turns, 0, i % turns, 0, 0))] * 4
    return pl.pallas_call(
        functools.partial(tick_kernel, relay, per_step, n_mp, apart, len(deps)),
        grid_spec=pltpu.PrefetchScalarGridSpec(
            num_scalar_prefetch=3,
            grid=(sections * turns,),
            in_specs=[whole, whole, weight, weight] + [pl.BlockSpec(memory_space=pl.ANY)] * len(deps),
            out_specs=slots_spec + [pl.BlockSpec((rows, width), lambda i, *_: (0, 0))],
            scratch_shapes=[pltpu.VMEM((width // block, rows, block), jnp.float32)],
        ),
        out_shape=slots + [jax.ShapeDtypeStruct((rows, width), jnp.bfloat16)],
        compiler_params=pltpu.CompilerParams(
            dimension_semantics=("arbitrary",), vmem_limit_bytes=56 * 1024 * 1024
        ),
        cost_estimate=pl.CostEstimate(
            flops=blocks * 10 * rows * block * block,
            bytes_accessed=blocks * block * block * 8 + rows * width * 6,
            transcendentals=blocks * rows * block,
        ),
        name=f"tick{relay}",
    )(lengths, idx_in, idx_out, section_in, out_grad, w_in, w_out, *deps)


def total(*parts):
    return functools.reduce(lambda a, b: a + b, [p.astype(jnp.float32) for p in parts])


def tie(value, *deps):
    any_space = pl.BlockSpec(memory_space=pl.ANY)
    return pl.pallas_call(
        lambda *refs: None,
        in_specs=[any_space] * (1 + len(deps)),
        out_specs=any_space,
        out_shape=jax.ShapeDtypeStruct(value.shape, value.dtype),
        input_output_aliases={0: 0},
        cost_estimate=pl.CostEstimate(flops=1000, bytes_accessed=1000, transcendentals=0),
        name="tie",
    )(value, *deps)


def flip_bit(value, axis, bit):
    return lax.ppermute(value, axis, [(i, i ^ bit) for i in range(lax.axis_size(axis))])


def from_behind(value, axis, distance):
    devices = range(lax.axis_size(axis))
    route = [(i - distance, i) for i in devices if i - distance in devices]
    return lax.ppermute(value, axis, route)


def rotate(parts, axis):
    n = lax.axis_size(axis)
    me = lax.axis_index(axis)
    got = []
    for k in range(n):
        part = lax.dynamic_index_in_dim(parts, lax.rem(me + k, n), 0, keepdims=False)
        got.append(part if k == 0 else lax.ppermute(part, axis, [(i, (i + k) % n) for i in range(n)]))
    return got


def by_source(parts, axis):
    n = len(parts)
    me = lax.axis_index(axis)
    stacked = jnp.stack(parts)
    return jnp.stack([lax.dynamic_index_in_dim(stacked, lax.rem(me - k + n, n), 0, keepdims=False) for k in range(n)])


def body(section_in, out_grad, lengths, w_in, w_out, idx_in, idx_out):
    sections, n_dp, n_mp = (lax.axis_size(a) for a in ("section", "dp", "mp"))
    args = (lengths.reshape(2), idx_in, idx_out, section_in, out_grad, w_in, w_out)

    def scatter(share):
        return lax.psum_scatter(share, "mp", scatter_dimension=0, tiled=True)

    a0, s0, a2, s2, share0 = tick(0, sections, n_dp, n_mp, False, [], *args)
    got0, got2 = flip_bit(s0, "dp", 1), flip_bit(s2, "dp", 1)
    sum0 = total(a2, got2).astype(jnp.bfloat16)
    came0 = flip_bit(sum0, "dp", 2)
    *slots, share1 = tick(1, sections, n_dp, n_mp, True, [sum0], *args)
    b0, t0, b2, t2 = (slots[2 * k:2 * k + 2] for k in range(4))
    hot0, hot2 = [flip_bit(v, "dp", 1) for v in t0], [flip_bit(v, "dp", 1) for v in t2]
    passed0 = from_behind(tie(scatter(share0), b0[0]), "section", -1)
    came1 = []
    for kept, hot in zip(b2, hot2):
        came1.append(flip_bit(total(tie(kept, came0, passed0, *hot0), hot).astype(jnp.bfloat16), "dp", 2))
    passed1 = from_behind(scatter(tie(share1, came0)), "section", 1)
    moved0 = rotate(total(a0, got0, came0).astype(jnp.bfloat16), "section")
    moved1 = []
    for kind in range(2):
        came = tie(came1[kind], passed1) if kind else came1[kind]
        moved1.append(rotate(total(b0[kind], hot0[kind], came).astype(jnp.bfloat16), "section"))
    moved1 = [jnp.stack(pair) for pair in zip(*moved1)]
    grads = total(by_source(moved0, "section"), jnp.flip(by_source(moved1, "section"), 0))
    return jnp.stack([passed0, passed1], axis=0)[:, None], grads[:, :, None]


def solution(mesh):
    placed = (
        P(None, "section", "dp", None),
        P(None, "section", "dp", None),
        P(None, "section", "dp"),
        P("section", None, "mp", None, None),
        P("section", None, "mp", None, None),
        P("section", None, "mp"),
        P("section", None, "mp"),
    )
    return jax.shard_map(
        body,
        mesh=mesh,
        in_specs=placed,
        out_specs=(
            P(None, "section", ("dp", "mp"), None),
            P(None, None, "mp", "section", "dp", None),
        ),
        check_vma=False,
    )
```

```python
import functools
import math

import jax
import jax.numpy as jnp
from jax import lax
from jax.experimental import pallas as pl
from jax.experimental.pallas import tpu as pltpu
from jax.sharding import PartitionSpec as P

SCALE = math.sqrt(2.0 / math.pi)
CUBIC = 0.044715
GROUP = 4


def tick_kernel(relay, per_step, n_mp, apart, n_deps, len_ref, idx_in_ref, idx_out_ref, x_ref, g_ref, w_in_ref, w_out_ref, *refs):
    *slot_refs, share_ref, acc_ref = refs[n_deps:]
    step = pl.program_id(0)
    me = lax.axis_index("dp")
    rows, block = x_ref.shape[0], w_in_ref.shape[-1]
    piece = slot_refs[0].shape[-2]
    live = lax.broadcasted_iota(jnp.int32, (rows, block), 0) < len_ref[relay]

    @pl.when(step == 0)
    def _():
        acc_ref[...] = jnp.zeros_like(acc_ref)

    odd, high = me % 2 == 1, me // 2 == 1

    def put(kind, i, value):
        value = value.astype(jnp.bfloat16)
        p = [value[q * piece:(q + 1) * piece] for q in range(4)]
        even = [jnp.where(odd, p[k + 1], p[k]) for k in (0, 2)]
        other = [jnp.where(odd, p[k], p[k + 1]) for k in (0, 2)]
        for slot, pair in ((0, even), (1, other)):
            for at, v in ((slot, jnp.where(high, pair[1], pair[0])), (slot + 2, jnp.where(high, pair[0], pair[1]))):
                if apart:
                    slot_refs[2 * at + kind][i] = v
                else:
                    slot_refs[at][kind, i] = v

    f32 = jnp.float32
    over_last = (((1,), (1,)), ((), ()))
    over_rows = (((0,), (0,)), ((), ()))
    for start in range(0, per_step, GROUP):
        group = range(start, min(start + GROUP, per_step))
        sources = [idx_in_ref[0, relay, step * per_step + i] for i in group]
        targets = [idx_out_ref[0, relay, step * per_step + i] for i in group]
        picked = [x_ref[:, pl.ds(pl.multiple_of(b * block, block), block)] for b in sources]
        back = [g_ref[:, pl.ds(pl.multiple_of(b * block, block), block)] for b in targets]
        back = [jnp.where(live, v, jnp.zeros_like(v)) for v in back]
        pre = [jnp.dot(v, w_in_ref[i], preferred_element_type=f32) for v, i in zip(picked, group)]
        back_pre = [lax.dot_general(v, w_out_ref[i], over_last, preferred_element_type=f32) for v, i in zip(back, group)]
        act, grad_pre = [], []
        for v, up in zip(pre, back_pre):
            square = v * v
            th = jnp.tanh(SCALE * (v + CUBIC * (square * v)))
            cdf = 0.5 * (1.0 + th)
            act.append((v * cdf).astype(jnp.bfloat16))
            slope = cdf + (0.5 * v) * ((1.0 - th) * (1.0 + th)) * (SCALE * (1.0 + (3.0 * CUBIC) * square))
            grad_pre.append((up * slope).astype(jnp.bfloat16))
        terms = [lax.dot_general(v, w_in_ref[i], over_last, preferred_element_type=f32) for v, i in zip(grad_pre, group)]
        grad_in = [lax.dot_general(a, v, over_rows, preferred_element_type=f32) for a, v in zip(picked, grad_pre)]
        grad_out = [lax.dot_general(a, v, over_rows, preferred_element_type=f32) for a, v in zip(act, back)]
        for i, b, term, g_in, g_out in zip(group, sources, terms, grad_in, grad_out):
            acc_ref[b] += term
            put(0, i, g_in)
            put(1, i, g_out)

    @pl.when(step == pl.num_programs(0) - 1)
    def _():
        share = rows // n_mp
        owned = live & (lax.broadcasted_iota(jnp.int32, (rows, block), 0) // share == lax.axis_index("mp"))
        for b in range(acc_ref.shape[0]):
            columns = slice(b * block, (b + 1) * block)
            held = g_ref[:, columns]
            held = jnp.where(owned, held, jnp.zeros_like(held)).astype(jnp.float32)
            share_ref[:, columns] = (acc_ref[b] + held).astype(jnp.bfloat16)


def tick(relay, sections, n_dp, n_mp, apart, deps, lengths, idx_in, idx_out, section_in, out_grad, w_in, w_out):
    rows, width = section_in.shape[2:]
    blocks, block = w_in.shape[2:4]
    per = blocks // sections
    per_step = math.gcd(per, 8)
    turns = per // per_step
    piece = block // n_dp
    whole = pl.BlockSpec((None, None, rows, width), lambda i, *_: (relay, 0, 0, 0))
    weight = pl.BlockSpec((None, None, per_step, block, block), lambda i, *_: (0, relay, i, 0, 0))
    if apart:
        slots = [jax.ShapeDtypeStruct((sections, per, piece, block), jnp.bfloat16)] * 8
        slots_spec = [pl.BlockSpec((None, per_step, piece, block), lambda i, *_: (i // turns, i % turns, 0, 0))] * 8
    else:
        slots = [jax.ShapeDtypeStruct((sections, 2, per, piece, block), jnp.bfloat16)] * 4
        slots_spec = [pl.BlockSpec((None, 2, per_step, piece, block), lambda i, *_: (i // turns, 0, i % turns, 0, 0))] * 4
    return pl.pallas_call(
        functools.partial(tick_kernel, relay, per_step, n_mp, apart, len(deps)),
        grid_spec=pltpu.PrefetchScalarGridSpec(
            num_scalar_prefetch=3,
            grid=(sections * turns,),
            in_specs=[whole, whole, weight, weight] + [pl.BlockSpec(memory_space=pl.ANY)] * len(deps),
            out_specs=slots_spec + [pl.BlockSpec((rows, width), lambda i, *_: (0, 0))],
            scratch_shapes=[pltpu.VMEM((width // block, rows, block), jnp.float32)],
        ),
        out_shape=slots + [jax.ShapeDtypeStruct((rows, width), jnp.bfloat16)],
        compiler_params=pltpu.CompilerParams(
            dimension_semantics=("arbitrary",), vmem_limit_bytes=56 * 1024 * 1024
        ),
        cost_estimate=pl.CostEstimate(
            flops=blocks * 10 * rows * block * block,
            bytes_accessed=blocks * block * block * 8 + rows * width * 6,
            transcendentals=blocks * rows * block,
        ),
        name=f"tick{relay}",
    )(lengths, idx_in, idx_out, section_in, out_grad, w_in, w_out, *deps)


def total(*parts):
    return functools.reduce(lambda a, b: a + b, [p.astype(jnp.float32) for p in parts])


def tie(value, *deps):
    any_space = pl.BlockSpec(memory_space=pl.ANY)
    return pl.pallas_call(
        lambda *refs: None,
        in_specs=[any_space] * (1 + len(deps)),
        out_specs=any_space,
        out_shape=jax.ShapeDtypeStruct(value.shape, value.dtype),
        input_output_aliases={0: 0},
        cost_estimate=pl.CostEstimate(flops=1000, bytes_accessed=1000, transcendentals=0),
        name="tie",
    )(value, *deps)


def flip_bit(value, axis, bit):
    return lax.ppermute(value, axis, [(i, i ^ bit) for i in range(lax.axis_size(axis))])


def from_behind(value, axis, distance):
    devices = range(lax.axis_size(axis))
    route = [(i - distance, i) for i in devices if i - distance in devices]
    return lax.ppermute(value, axis, route)


def rotate(parts, axis):
    n = lax.axis_size(axis)
    me = lax.axis_index(axis)
    got = []
    for k in range(n):
        part = lax.dynamic_index_in_dim(parts, lax.rem(me + k, n), 0, keepdims=False)
        got.append(part if k == 0 else lax.ppermute(part, axis, [(i, (i + k) % n) for i in range(n)]))
    return got


def by_source(parts, axis):
    n = len(parts)
    me = lax.axis_index(axis)
    stacked = jnp.stack(parts)
    return jnp.stack([lax.dynamic_index_in_dim(stacked, lax.rem(me - k + n, n), 0, keepdims=False) for k in range(n)])


def body(section_in, out_grad, lengths, w_in, w_out, idx_in, idx_out):
    sections, n_dp, n_mp = (lax.axis_size(a) for a in ("section", "dp", "mp"))
    args = (lengths.reshape(2), idx_in, idx_out, section_in, out_grad, w_in, w_out)

    def scatter(share):
        return lax.psum_scatter(share, "mp", scatter_dimension=0, tiled=True)

    def core_pair(slots):
        keep0, send0, keep2, send2 = (slots[2 * k:2 * k + 2] for k in range(4))
        got0, got2 = [flip_bit(v, "dp", 1) for v in send0], [flip_bit(v, "dp", 1) for v in send2]
        return keep0, got0, keep2, got2

    def on_section(kept, got, came):
        return rotate(total(kept, got, came).astype(jnp.bfloat16), "section")

    *slots, share0 = tick(0, sections, n_dp, n_mp, True, [], *args)
    a0, got0, a2, got2 = core_pair(slots)
    sums = [total(tie(k, *got0), g).astype(jnp.bfloat16) for k, g in zip(a2, got2)]
    came0 = [flip_bit(v, "dp", 2) for v in sums]
    *slots, share1 = tick(1, sections, n_dp, n_mp, True, sums, *args)
    b0, hot0, b2, hot2 = core_pair(slots)
    first = on_section(a0[0], got0[0], came0[0])
    deps = [came0[1], *first[1:], *hot0]
    came1 = [flip_bit(total(tie(k, *deps), g).astype(jnp.bfloat16), "dp", 2) for k, g in zip(b2, hot2)]
    second = on_section(a0[1], got0[1], came0[1])
    passed0 = from_behind(scatter(share0), "section", -1)
    passed1 = from_behind(scatter(tie(share1, *first[1:])), "section", 1)
    third = on_section(b0[0], hot0[0], tie(came1[0], passed0))
    fourth = on_section(b0[1], hot0[1], tie(came1[1], passed1))
    moved0, moved1 = ([jnp.stack(pair) for pair in zip(*pairs)] for pairs in ((first, second), (third, fourth)))
    grads = total(by_source(moved0, "section"), jnp.flip(by_source(moved1, "section"), 0))
    return jnp.stack([passed0, passed1], axis=0)[:, None], grads[:, :, None]


def solution(mesh):
    placed = (
        P(None, "section", "dp", None),
        P(None, "section", "dp", None),
        P(None, "section", "dp"),
        P("section", None, "mp", None, None),
        P("section", None, "mp", None, None),
        P("section", None, "mp"),
        P("section", None, "mp"),
    )
    return jax.shard_map(
        body,
        mesh=mesh,
        in_specs=placed,
        out_specs=(
            P(None, "section", ("dp", "mp"), None),
            P(None, None, "mp", "section", "dp", None),
        ),
        check_vma=False,
    )
```

```python
import functools
import math

import jax
import jax.numpy as jnp
from jax import lax
from jax.experimental import pallas as pl
from jax.experimental.pallas import tpu as pltpu
from jax.sharding import PartitionSpec as P

SCALE = math.sqrt(2.0 / math.pi)
CUBIC = 0.044715
GROUP = 4


def tick_kernel(relay, per_step, n_mp, apart, n_deps, len_ref, idx_in_ref, idx_out_ref, x_ref, g_ref, w_in_ref, w_out_ref, *refs):
    *slot_refs, share_ref, acc_ref = refs[n_deps:]
    step = pl.program_id(0)
    me = lax.axis_index("dp")
    rows, block = x_ref.shape[0], w_in_ref.shape[-1]
    piece = slot_refs[0].shape[-2]
    live = lax.broadcasted_iota(jnp.int32, (rows, block), 0) < len_ref[relay]

    @pl.when(step == 0)
    def _():
        acc_ref[...] = jnp.zeros_like(acc_ref)

    odd, high = me % 2 == 1, me // 2 == 1

    def put(kind, i, value):
        value = value.astype(jnp.bfloat16)
        p = [value[q * piece:(q + 1) * piece] for q in range(4)]
        even = [jnp.where(odd, p[k + 1], p[k]) for k in (0, 2)]
        other = [jnp.where(odd, p[k], p[k + 1]) for k in (0, 2)]
        for slot, pair in ((0, even), (1, other)):
            for at, v in ((slot, jnp.where(high, pair[1], pair[0])), (slot + 2, jnp.where(high, pair[0], pair[1]))):
                if apart:
                    slot_refs[2 * at + kind][i] = v
                else:
                    slot_refs[at][kind, i] = v

    f32 = jnp.float32
    over_last = (((1,), (1,)), ((), ()))
    over_rows = (((0,), (0,)), ((), ()))
    for start in range(0, per_step, GROUP):
        group = range(start, min(start + GROUP, per_step))
        sources = [idx_in_ref[0, relay, step * per_step + i] for i in group]
        targets = [idx_out_ref[0, relay, step * per_step + i] for i in group]
        picked = [x_ref[:, pl.ds(pl.multiple_of(b * block, block), block)] for b in sources]
        back = [g_ref[:, pl.ds(pl.multiple_of(b * block, block), block)] for b in targets]
        back = [jnp.where(live, v, jnp.zeros_like(v)) for v in back]
        pre = [jnp.dot(v, w_in_ref[i], preferred_element_type=f32) for v, i in zip(picked, group)]
        back_pre = [lax.dot_general(v, w_out_ref[i], over_last, preferred_element_type=f32) for v, i in zip(back, group)]
        act, grad_pre = [], []
        for v, up in zip(pre, back_pre):
            square = v * v
            th = jnp.tanh(SCALE * (v + CUBIC * (square * v)))
            cdf = 0.5 * (1.0 + th)
            act.append((v * cdf).astype(jnp.bfloat16))
            slope = cdf + (0.5 * v) * ((1.0 - th) * (1.0 + th)) * (SCALE * (1.0 + (3.0 * CUBIC) * square))
            grad_pre.append((up * slope).astype(jnp.bfloat16))
        terms = [lax.dot_general(v, w_in_ref[i], over_last, preferred_element_type=f32) for v, i in zip(grad_pre, group)]
        grad_in = [lax.dot_general(a, v, over_rows, preferred_element_type=f32) for a, v in zip(picked, grad_pre)]
        grad_out = [lax.dot_general(a, v, over_rows, preferred_element_type=f32) for a, v in zip(act, back)]
        for i, b, term, g_in, g_out in zip(group, sources, terms, grad_in, grad_out):
            acc_ref[b] += term
            put(0, i, g_in)
            put(1, i, g_out)

    @pl.when(step == pl.num_programs(0) - 1)
    def _():
        share = rows // n_mp
        owned = live & (lax.broadcasted_iota(jnp.int32, (rows, block), 0) // share == lax.axis_index("mp"))
        for b in range(acc_ref.shape[0]):
            columns = slice(b * block, (b + 1) * block)
            held = g_ref[:, columns]
            held = jnp.where(owned, held, jnp.zeros_like(held)).astype(jnp.float32)
            share_ref[:, columns] = (acc_ref[b] + held).astype(jnp.bfloat16)


def tick(relay, sections, n_dp, n_mp, apart, deps, lengths, idx_in, idx_out, section_in, out_grad, w_in, w_out):
    rows, width = section_in.shape[2:]
    blocks, block = w_in.shape[2:4]
    per = blocks // sections
    per_step = math.gcd(per, 8)
    turns = per // per_step
    piece = block // n_dp
    whole = pl.BlockSpec((None, None, rows, width), lambda i, *_: (relay, 0, 0, 0))
    weight = pl.BlockSpec((None, None, per_step, block, block), lambda i, *_: (0, relay, i, 0, 0))
    if apart:
        slots = [jax.ShapeDtypeStruct((sections, per, piece, block), jnp.bfloat16)] * 8
        slots_spec = [pl.BlockSpec((None, per_step, piece, block), lambda i, *_: (i // turns, i % turns, 0, 0))] * 8
    else:
        slots = [jax.ShapeDtypeStruct((sections, 2, per, piece, block), jnp.bfloat16)] * 4
        slots_spec = [pl.BlockSpec((None, 2, per_step, piece, block), lambda i, *_: (i // turns, 0, i % turns, 0, 0))] * 4
    return pl.pallas_call(
        functools.partial(tick_kernel, relay, per_step, n_mp, apart, len(deps)),
        grid_spec=pltpu.PrefetchScalarGridSpec(
            num_scalar_prefetch=3,
            grid=(sections * turns,),
            in_specs=[whole, whole, weight, weight] + [pl.BlockSpec(memory_space=pl.ANY)] * len(deps),
            out_specs=slots_spec + [pl.BlockSpec((rows, width), lambda i, *_: (0, 0))],
            scratch_shapes=[pltpu.VMEM((width // block, rows, block), jnp.float32)],
        ),
        out_shape=slots + [jax.ShapeDtypeStruct((rows, width), jnp.bfloat16)],
        compiler_params=pltpu.CompilerParams(
            dimension_semantics=("arbitrary",), vmem_limit_bytes=56 * 1024 * 1024
        ),
        cost_estimate=pl.CostEstimate(
            flops=blocks * 10 * rows * block * block,
            bytes_accessed=blocks * block * block * 8 + rows * width * 6,
            transcendentals=blocks * rows * block,
        ),
        name=f"tick{relay}",
    )(lengths, idx_in, idx_out, section_in, out_grad, w_in, w_out, *deps)


def total(*parts):
    return functools.reduce(lambda a, b: a + b, [p.astype(jnp.float32) for p in parts])


def tie(value, *deps):
    any_space = pl.BlockSpec(memory_space=pl.ANY)
    return pl.pallas_call(
        lambda *refs: None,
        in_specs=[any_space] * (1 + len(deps)),
        out_specs=any_space,
        out_shape=jax.ShapeDtypeStruct(value.shape, value.dtype),
        input_output_aliases={0: 0},
        cost_estimate=pl.CostEstimate(flops=1000, bytes_accessed=1000, transcendentals=0),
        name="tie",
    )(value, *deps)


def flip_bit(value, axis, bit):
    return lax.ppermute(value, axis, [(i, i ^ bit) for i in range(lax.axis_size(axis))])


def from_behind(value, axis, distance):
    devices = range(lax.axis_size(axis))
    route = [(i - distance, i) for i in devices if i - distance in devices]
    return lax.ppermute(value, axis, route)


def rotate(parts, axis):
    n = lax.axis_size(axis)
    me = lax.axis_index(axis)
    got = []
    for k in range(n):
        part = lax.dynamic_index_in_dim(parts, lax.rem(me + k, n), 0, keepdims=False)
        got.append(part if k == 0 else lax.ppermute(part, axis, [(i, (i + k) % n) for i in range(n)]))
    return got


def by_source(parts, axis):
    n = len(parts)
    me = lax.axis_index(axis)
    stacked = jnp.stack(parts)
    return jnp.stack([lax.dynamic_index_in_dim(stacked, lax.rem(me - k + n, n), 0, keepdims=False) for k in range(n)])


def body(section_in, out_grad, lengths, w_in, w_out, idx_in, idx_out):
    sections, n_dp, n_mp = (lax.axis_size(a) for a in ("section", "dp", "mp"))
    args = (lengths.reshape(2), idx_in, idx_out, section_in, out_grad, w_in, w_out)

    def scatter(share):
        return lax.psum_scatter(share, "mp", scatter_dimension=0, tiled=True)

    def core_pair(slots):
        keep0, send0, keep2, send2 = (slots[2 * k:2 * k + 2] for k in range(4))
        got0, got2 = [flip_bit(v, "dp", 1) for v in send0], [flip_bit(v, "dp", 1) for v in send2]
        return keep0, got0, keep2, got2

    def on_section(kept, got, came):
        return rotate(total(kept, got, came).astype(jnp.bfloat16), "section")

    *slots, share0 = tick(0, sections, n_dp, n_mp, True, [], *args)
    a0, got0, a2, got2 = core_pair(slots)
    sums = [total(tie(k, *got0), g).astype(jnp.bfloat16) for k, g in zip(a2, got2)]
    came0 = [flip_bit(v, "dp", 2) for v in sums]
    *slots, share1 = tick(1, sections, n_dp, n_mp, True, sums, *args)
    b0, hot0, b2, hot2 = core_pair(slots)
    first = on_section(a0[0], got0[0], tie(came0[0], sums[1]))
    deps = [came0[1], *first[1:]]
    came1 = [flip_bit(total(tie(k, *deps), g).astype(jnp.bfloat16), "dp", 2) for k, g in zip(b2, hot2)]
    second = on_section(tie(a0[1], *hot0), got0[1], came0[1])
    passed0 = from_behind(scatter(share0), "section", -1)
    passed1 = from_behind(scatter(tie(share1, *first[1:])), "section", 1)
    third = on_section(b0[0], hot0[0], tie(came1[0], passed0))
    fourth = on_section(b0[1], hot0[1], tie(came1[1], passed1))
    moved0, moved1 = ([jnp.stack(pair) for pair in zip(*pairs)] for pairs in ((first, second), (third, fourth)))
    grads = total(by_source(moved0, "section"), jnp.flip(by_source(moved1, "section"), 0))
    return jnp.stack([passed0, passed1], axis=0)[:, None], grads[:, :, None]


def solution(mesh):
    placed = (
        P(None, "section", "dp", None),
        P(None, "section", "dp", None),
        P(None, "section", "dp"),
        P("section", None, "mp", None, None),
        P("section", None, "mp", None, None),
        P("section", None, "mp"),
        P("section", None, "mp"),
    )
    return jax.shard_map(
        body,
        mesh=mesh,
        in_specs=placed,
        out_specs=(
            P(None, "section", ("dp", "mp"), None),
            P(None, None, "mp", "section", "dp", None),
        ),
        check_vma=False,
    )
```

```python
import functools
import math

import jax
import jax.numpy as jnp
from jax import lax
from jax.experimental import pallas as pl
from jax.experimental.pallas import tpu as pltpu
from jax.sharding import PartitionSpec as P

SCALE = math.sqrt(2.0 / math.pi)
CUBIC = 0.044715
GROUP = 4


def tick_kernel(relay, per_step, n_mp, n_deps, len_ref, idx_in_ref, idx_out_ref, x_ref, g_ref, w_in_ref, w_out_ref, *refs):
    if relay:
        g0_ref, w0_ref, gp0_ref = refs[:3]
        *slot_refs, share0_ref, share_ref, acc0_ref, acc_ref = refs[3 + n_deps:]
    else:
        *slot_refs, gp_ref = refs[n_deps:]
    step = pl.program_id(0)
    me = lax.axis_index("dp")
    rows, block = x_ref.shape[0], w_in_ref.shape[-1]
    piece = slot_refs[0].shape[2]
    live = lax.broadcasted_iota(jnp.int32, (rows, block), 0) < len_ref[relay]

    if relay:
        @pl.when(step == 0)
        def _():
            acc_ref[...] = jnp.zeros_like(acc_ref)
            acc0_ref[...] = jnp.zeros_like(acc0_ref)

    odd, high = me % 2 == 1, me // 2 == 1

    def put(kind, i, value):
        value = value.astype(jnp.bfloat16)
        p = [value[q * piece:(q + 1) * piece] for q in range(4)]
        even = [jnp.where(odd, p[k + 1], p[k]) for k in (0, 2)]
        other = [jnp.where(odd, p[k], p[k + 1]) for k in (0, 2)]
        for slot, pair in ((0, even), (1, other)):
            slot_refs[slot][kind, i] = jnp.where(high, pair[1], pair[0])
            slot_refs[slot + 2][kind, i] = jnp.where(high, pair[0], pair[1])

    f32 = jnp.float32
    over_last = (((1,), (1,)), ((), ()))
    over_rows = (((0,), (0,)), ((), ()))
    for start in range(0, per_step, GROUP):
        group = range(start, min(start + GROUP, per_step))
        sources = [idx_in_ref[0, relay, step * per_step + i] for i in group]
        targets = [idx_out_ref[0, relay, step * per_step + i] for i in group]
        picked = [x_ref[:, pl.ds(pl.multiple_of(b * block, block), block)] for b in sources]
        back = [g_ref[:, pl.ds(pl.multiple_of(b * block, block), block)] for b in targets]
        back = [jnp.where(live, v, jnp.zeros_like(v)) for v in back]
        pre = [jnp.dot(v, w_in_ref[i], preferred_element_type=f32) for v, i in zip(picked, group)]
        back_pre = [lax.dot_general(v, w_out_ref[i], over_last, preferred_element_type=f32) for v, i in zip(back, group)]
        act, grad_pre = [], []
        for v, up in zip(pre, back_pre):
            square = v * v
            th = jnp.tanh(SCALE * (v + CUBIC * (square * v)))
            cdf = 0.5 * (1.0 + th)
            act.append((v * cdf).astype(jnp.bfloat16))
            slope = cdf + (0.5 * v) * ((1.0 - th) * (1.0 + th)) * (SCALE * (1.0 + (3.0 * CUBIC) * square))
            grad_pre.append((up * slope).astype(jnp.bfloat16))
        if relay:
            terms = [lax.dot_general(v, w_in_ref[i], over_last, preferred_element_type=f32) for v, i in zip(grad_pre, group)]
            sources0 = [idx_in_ref[0, 0, step * per_step + i] for i in group]
            terms0 = [lax.dot_general(gp0_ref[i], w0_ref[i], over_last, preferred_element_type=f32) for i in group]
        grad_in = [lax.dot_general(a, v, over_rows, preferred_element_type=f32) for a, v in zip(picked, grad_pre)]
        grad_out = [lax.dot_general(a, v, over_rows, preferred_element_type=f32) for a, v in zip(act, back)]
        if relay:
            for b, term, b0, term0 in zip(sources, terms, sources0, terms0):
                acc_ref[b] += term
                acc0_ref[b0] += term0
        else:
            for i, v in zip(group, grad_pre):
                gp_ref[i] = v
        for i, g_in, g_out in zip(group, grad_in, grad_out):
            put(0, i, g_in)
            put(1, i, g_out)

    if not relay:
        return

    @pl.when(step == pl.num_programs(0) - 1)
    def _():
        share = rows // n_mp
        owned = (lax.broadcasted_iota(jnp.int32, (rows, block), 0) // share == lax.axis_index("mp"))
        live0 = lax.broadcasted_iota(jnp.int32, (rows, block), 0) < len_ref[0]
        for rows_live, held_ref, sum_ref, out_ref in ((live0, g0_ref, acc0_ref, share0_ref), (live, g_ref, acc_ref, share_ref)):
            for b in range(acc_ref.shape[0]):
                columns = slice(b * block, (b + 1) * block)
                held = held_ref[:, columns]
                held = jnp.where(rows_live & owned, held, jnp.zeros_like(held)).astype(jnp.float32)
                out_ref[:, columns] = (sum_ref[b] + held).astype(jnp.bfloat16)


def tick(relay, sections, n_dp, n_mp, deps, gp0, lengths, idx_in, idx_out, section_in, out_grad, w_in, w_out):
    rows, width = section_in.shape[2:]
    blocks, block = w_in.shape[2:4]
    per = blocks // sections
    per_step = math.gcd(per, 8)
    turns = per // per_step
    piece = block // n_dp
    whole = pl.BlockSpec((None, None, rows, width), lambda i, *_: (relay, 0, 0, 0))
    weight = pl.BlockSpec((None, None, per_step, block, block), lambda i, *_: (0, relay, i, 0, 0))
    slots = jax.ShapeDtypeStruct((sections, 2, per, piece, block), jnp.bfloat16)
    slots_spec = pl.BlockSpec((None, 2, per_step, piece, block), lambda i, *_: (i // turns, 0, i % turns, 0, 0))
    terms_spec = pl.BlockSpec((per_step, rows, block), lambda i, *_: (i, 0, 0))
    acc = pltpu.VMEM((width // block, rows, block), jnp.float32)
    share_spec = pl.BlockSpec((rows, width), lambda i, *_: (0, 0))
    share = jax.ShapeDtypeStruct((rows, width), jnp.bfloat16)
    extra_specs, extra = [], []
    if relay:
        extra_specs = [
            pl.BlockSpec((None, None, rows, width), lambda i, *_: (0, 0, 0, 0)),
            pl.BlockSpec((None, None, per_step, block, block), lambda i, *_: (0, 0, i, 0, 0)),
            terms_spec,
        ]
        extra = [out_grad, w_in, gp0]
    return pl.pallas_call(
        functools.partial(tick_kernel, relay, per_step, n_mp, len(deps)),
        grid_spec=pltpu.PrefetchScalarGridSpec(
            num_scalar_prefetch=3,
            grid=(sections * turns,),
            in_specs=[whole, whole, weight, weight] + extra_specs + [pl.BlockSpec(memory_space=pl.ANY)] * len(deps),
            out_specs=[slots_spec] * 4 + ([share_spec] * 2 if relay else [terms_spec]),
            scratch_shapes=[acc] * 2 if relay else [],
        ),
        out_shape=[slots] * 4
        + ([share] * 2 if relay else [jax.ShapeDtypeStruct((blocks, rows, block), jnp.bfloat16)]),
        compiler_params=pltpu.CompilerParams(
            dimension_semantics=("arbitrary",), vmem_limit_bytes=58 * 1024 * 1024
        ),
        cost_estimate=pl.CostEstimate(
            flops=blocks * 10 * rows * block * block,
            bytes_accessed=blocks * block * block * 8 + rows * width * 6,
            transcendentals=blocks * rows * block,
        ),
        name=f"tick{relay}",
    )(lengths, idx_in, idx_out, section_in, out_grad, w_in, w_out, *extra, *deps)


def total(*parts):
    return functools.reduce(lambda a, b: a + b, [p.astype(jnp.float32) for p in parts])


def tie(value, *deps):
    any_space = pl.BlockSpec(memory_space=pl.ANY)
    return pl.pallas_call(
        lambda *refs: None,
        in_specs=[any_space] * (1 + len(deps)),
        out_specs=any_space,
        out_shape=jax.ShapeDtypeStruct(value.shape, value.dtype),
        input_output_aliases={0: 0},
        cost_estimate=pl.CostEstimate(flops=1000, bytes_accessed=1000, transcendentals=0),
        name="tie",
    )(value, *deps)


def flip_bit(value, axis, bit):
    return lax.ppermute(value, axis, [(i, i ^ bit) for i in range(lax.axis_size(axis))])


def from_behind(value, axis, distance):
    devices = range(lax.axis_size(axis))
    route = [(i - distance, i) for i in devices if i - distance in devices]
    return lax.ppermute(value, axis, route)


def rotate(parts, axis):
    n = lax.axis_size(axis)
    me = lax.axis_index(axis)
    got = []
    for k in range(n):
        part = lax.dynamic_index_in_dim(parts, lax.rem(me + k, n), 0, keepdims=False)
        got.append(part if k == 0 else lax.ppermute(part, axis, [(i, (i + k) % n) for i in range(n)]))
    return got


def by_source(parts, axis):
    n = len(parts)
    me = lax.axis_index(axis)
    stacked = jnp.stack(parts)
    return jnp.stack([lax.dynamic_index_in_dim(stacked, lax.rem(me - k + n, n), 0, keepdims=False) for k in range(n)])


def body(section_in, out_grad, lengths, w_in, w_out, idx_in, idx_out):
    sections, n_dp, n_mp = (lax.axis_size(a) for a in ("section", "dp", "mp"))
    args = (lengths.reshape(2), idx_in, idx_out, section_in, out_grad, w_in, w_out)

    def scatter(share):
        return lax.psum_scatter(share, "mp", scatter_dimension=0, tiled=True)

    a0, s0, a2, s2, gp0 = tick(0, sections, n_dp, n_mp, [], None, *args)
    got0, got2 = flip_bit(s0, "dp", 1), flip_bit(s2, "dp", 1)
    sum0 = total(a2, got2).astype(jnp.bfloat16)
    came0 = flip_bit(sum0, "dp", 2)
    b0, t0, b2, t2, share0, share1 = tick(1, sections, n_dp, n_mp, [sum0], gp0, *args)
    hot0, hot2 = flip_bit(t0, "dp", 1), flip_bit(t2, "dp", 1)
    dx0 = scatter(share0)
    sum1 = total(tie(b2, came0), hot2).astype(jnp.bfloat16)
    came1 = flip_bit(sum1, "dp", 2)
    dx1 = scatter(tie(share1, came0))
    moved0 = rotate(total(a0, got0, came0).astype(jnp.bfloat16), "section")
    passed0 = from_behind(dx0, "section", -1)
    passed1 = from_behind(dx1, "section", 1)
    moved1 = rotate(total(b0, hot0, came1).astype(jnp.bfloat16), "section")
    grads = total(by_source(moved0, "section"), jnp.flip(by_source(moved1, "section"), 0))
    return jnp.stack([passed0, passed1], axis=0)[:, None], grads[:, :, None]


def solution(mesh):
    placed = (
        P(None, "section", "dp", None),
        P(None, "section", "dp", None),
        P(None, "section", "dp"),
        P("section", None, "mp", None, None),
        P("section", None, "mp", None, None),
        P("section", None, "mp"),
        P("section", None, "mp"),
    )
    return jax.shard_map(
        body,
        mesh=mesh,
        in_specs=placed,
        out_specs=(
            P(None, "section", ("dp", "mp"), None),
            P(None, None, "mp", "section", "dp", None),
        ),
        check_vma=False,
    )
```

```python
import functools
import math

import jax
import jax.numpy as jnp
from jax import lax
from jax.experimental import pallas as pl
from jax.experimental.pallas import tpu as pltpu
from jax.sharding import PartitionSpec as P

SCALE = math.sqrt(2.0 / math.pi)
CUBIC = 0.044715
GROUP = 4


def tick_kernel(relay, per_step, n_mp, n_deps, len_ref, idx_in_ref, idx_out_ref, x_ref, g_ref, w_in_ref, w_out_ref, *refs):
    *slot_refs, share_ref, acc_ref = refs[n_deps:]
    step = pl.program_id(0)
    me = lax.axis_index("dp")
    rows, block = x_ref.shape[0], w_in_ref.shape[-1]
    piece = slot_refs[0].shape[2]
    live = lax.broadcasted_iota(jnp.int32, (rows, block), 0) < len_ref[relay]

    @pl.when(step == 0)
    def _():
        acc_ref[...] = jnp.zeros_like(acc_ref)

    odd, high = me % 2 == 1, me // 2 == 1

    def put(kind, i, value):
        value = value.astype(jnp.bfloat16)
        p = [value[q * piece:(q + 1) * piece] for q in range(4)]
        even = [jnp.where(odd, p[k + 1], p[k]) for k in (0, 2)]
        other = [jnp.where(odd, p[k], p[k + 1]) for k in (0, 2)]
        for slot, pair in ((0, even), (1, other)):
            slot_refs[slot][kind, i] = jnp.where(high, pair[1], pair[0])
            slot_refs[slot + 2][kind, i] = jnp.where(high, pair[0], pair[1])

    f32 = jnp.float32
    over_last = (((1,), (1,)), ((), ()))
    over_rows = (((0,), (0,)), ((), ()))
    for start in range(0, per_step, GROUP):
        group = range(start, min(start + GROUP, per_step))
        sources = [idx_in_ref[0, relay, step * per_step + i] for i in group]
        targets = [idx_out_ref[0, relay, step * per_step + i] for i in group]
        picked = [x_ref[:, pl.ds(pl.multiple_of(b * block, block), block)] for b in sources]
        back = [g_ref[:, pl.ds(pl.multiple_of(b * block, block), block)] for b in targets]
        back = [jnp.where(live, v, jnp.zeros_like(v)) for v in back]
        pre = [jnp.dot(v, w_in_ref[i], preferred_element_type=f32) for v, i in zip(picked, group)]
        back_pre = [lax.dot_general(v, w_out_ref[i], over_last, preferred_element_type=f32) for v, i in zip(back, group)]
        act, grad_pre = [], []
        for v, up in zip(pre, back_pre):
            square = v * v
            th = jnp.tanh(SCALE * (v + CUBIC * (square * v)))
            cdf = 0.5 * (1.0 + th)
            act.append((v * cdf).astype(jnp.bfloat16))
            slope = cdf + (0.5 * v) * ((1.0 - th) * (1.0 + th)) * (SCALE * (1.0 + (3.0 * CUBIC) * square))
            grad_pre.append((up * slope).astype(jnp.bfloat16))
        terms = [lax.dot_general(v, w_in_ref[i], over_last, preferred_element_type=f32) for v, i in zip(grad_pre, group)]
        grad_in = [lax.dot_general(a, v, over_rows, preferred_element_type=f32) for a, v in zip(picked, grad_pre)]
        grad_out = [lax.dot_general(a, v, over_rows, preferred_element_type=f32) for a, v in zip(act, back)]
        for i, b, term, g_in, g_out in zip(group, sources, terms, grad_in, grad_out):
            acc_ref[b] += term
            put(0, i, g_in)
            put(1, i, g_out)

    @pl.when(step == pl.num_programs(0) - 1)
    def _():
        share = rows // n_mp
        owned = live & (lax.broadcasted_iota(jnp.int32, (rows, block), 0) // share == lax.axis_index("mp"))
        for b in range(acc_ref.shape[0]):
            columns = slice(b * block, (b + 1) * block)
            held = g_ref[:, columns]
            held = jnp.where(owned, held, jnp.zeros_like(held)).astype(jnp.float32)
            share_ref[:, columns] = (acc_ref[b] + held).astype(jnp.bfloat16)


def tick(relay, sections, n_dp, n_mp, deps, lengths, idx_in, idx_out, section_in, out_grad, w_in, w_out):
    rows, width = section_in.shape[2:]
    blocks, block = w_in.shape[2:4]
    per = blocks // sections
    per_step = math.gcd(per, 12)
    turns = per // per_step
    piece = block // n_dp
    whole = pl.BlockSpec((None, None, rows, width), lambda i, *_: (relay, 0, 0, 0))
    weight = pl.BlockSpec((None, None, per_step, block, block), lambda i, *_: (0, relay, i, 0, 0))
    slots = jax.ShapeDtypeStruct((sections, 2, per, piece, block), jnp.bfloat16)
    slots_spec = pl.BlockSpec((None, 2, per_step, piece, block), lambda i, *_: (i // turns, 0, i % turns, 0, 0))
    return pl.pallas_call(
        functools.partial(tick_kernel, relay, per_step, n_mp, len(deps)),
        grid_spec=pltpu.PrefetchScalarGridSpec(
            num_scalar_prefetch=3,
            grid=(sections * turns,),
            in_specs=[whole, whole, weight, weight] + [pl.BlockSpec(memory_space=pl.ANY)] * len(deps),
            out_specs=[slots_spec] * 4 + [pl.BlockSpec((rows, width), lambda i, *_: (0, 0))],
            scratch_shapes=[pltpu.VMEM((width // block, rows, block), jnp.float32)],
        ),
        out_shape=[slots] * 4 + [jax.ShapeDtypeStruct((rows, width), jnp.bfloat16)],
        compiler_params=pltpu.CompilerParams(
            dimension_semantics=("arbitrary",), vmem_limit_bytes=56 * 1024 * 1024
        ),
        cost_estimate=pl.CostEstimate(
            flops=blocks * 10 * rows * block * block,
            bytes_accessed=blocks * block * block * 8 + rows * width * 6,
            transcendentals=blocks * rows * block,
        ),
        name=f"tick{relay}",
    )(lengths, idx_in, idx_out, section_in, out_grad, w_in, w_out, *deps)


def total(*parts):
    return functools.reduce(lambda a, b: a + b, [p.astype(jnp.float32) for p in parts])


def tie(value, *deps):
    any_space = pl.BlockSpec(memory_space=pl.ANY)
    return pl.pallas_call(
        lambda *refs: None,
        in_specs=[any_space] * (1 + len(deps)),
        out_specs=any_space,
        out_shape=jax.ShapeDtypeStruct(value.shape, value.dtype),
        input_output_aliases={0: 0},
        cost_estimate=pl.CostEstimate(flops=1000, bytes_accessed=1000, transcendentals=0),
        name="tie",
    )(value, *deps)


def flip_bit(value, axis, bit):
    return lax.ppermute(value, axis, [(i, i ^ bit) for i in range(lax.axis_size(axis))])


def from_behind(value, axis, distance):
    devices = range(lax.axis_size(axis))
    route = [(i - distance, i) for i in devices if i - distance in devices]
    return lax.ppermute(value, axis, route)


def rotate(parts, axis):
    n = lax.axis_size(axis)
    me = lax.axis_index(axis)
    got = []
    for k in range(n):
        part = lax.dynamic_index_in_dim(parts, lax.rem(me + k, n), 0, keepdims=False)
        got.append(part if k == 0 else lax.ppermute(part, axis, [(i, (i + k) % n) for i in range(n)]))
    return got


def by_source(parts, axis):
    n = len(parts)
    me = lax.axis_index(axis)
    stacked = jnp.stack(parts)
    return jnp.stack([lax.dynamic_index_in_dim(stacked, lax.rem(me - k + n, n), 0, keepdims=False) for k in range(n)])


def body(section_in, out_grad, lengths, w_in, w_out, idx_in, idx_out):
    sections, n_dp, n_mp = (lax.axis_size(a) for a in ("section", "dp", "mp"))
    args = (lengths.reshape(2), idx_in, idx_out, section_in, out_grad, w_in, w_out)

    def scatter(share):
        return lax.psum_scatter(share, "mp", scatter_dimension=0, tiled=True)

    a0, s0, a2, s2, share0 = tick(0, sections, n_dp, n_mp, [], *args)
    got0, got2 = flip_bit(s0, "dp", 1), flip_bit(s2, "dp", 1)
    sum0 = total(a2, got2).astype(jnp.bfloat16)
    came0 = flip_bit(sum0, "dp", 2)
    b0, t0, b2, t2, share1 = tick(1, sections, n_dp, n_mp, [sum0], *args)
    hot0, hot2 = flip_bit(t0, "dp", 1), flip_bit(t2, "dp", 1)
    dx0 = scatter(share0)
    sum1 = total(tie(b2, came0), hot2).astype(jnp.bfloat16)
    came1 = flip_bit(sum1, "dp", 2)
    dx1 = scatter(tie(share1, came0))
    moved0 = rotate(total(a0, got0, came0).astype(jnp.bfloat16), "section")
    passed0 = from_behind(dx0, "section", -1)
    passed1 = from_behind(dx1, "section", 1)
    moved1 = rotate(total(b0, hot0, came1).astype(jnp.bfloat16), "section")
    grads = total(by_source(moved0, "section"), jnp.flip(by_source(moved1, "section"), 0))
    return jnp.stack([passed0, passed1], axis=0)[:, None], grads[:, :, None]


def solution(mesh):
    placed = (
        P(None, "section", "dp", None),
        P(None, "section", "dp", None),
        P(None, "section", "dp"),
        P("section", None, "mp", None, None),
        P("section", None, "mp", None, None),
        P("section", None, "mp"),
        P("section", None, "mp"),
    )
    return jax.shard_map(
        body,
        mesh=mesh,
        in_specs=placed,
        out_specs=(
            P(None, "section", ("dp", "mp"), None),
            P(None, None, "mp", "section", "dp", None),
        ),
        check_vma=False,
    )
```

```python
import functools
import math

import jax
import jax.numpy as jnp
from jax import lax
from jax.experimental import pallas as pl
from jax.experimental.pallas import tpu as pltpu
from jax.sharding import PartitionSpec as P

SCALE = math.sqrt(2.0 / math.pi)
CUBIC = 0.044715
GROUP = 4


def tick_kernel(relay, per_step, n_mp, n_deps, len_ref, idx_in_ref, idx_out_ref, x_ref, g_ref, w_in_ref, w_out_ref, *refs):
    *slot_refs, share_ref, acc_ref = refs[n_deps:]
    step = pl.program_id(0)
    me = lax.axis_index("dp")
    rows, block = x_ref.shape[0], w_in_ref.shape[-1]
    piece = slot_refs[0].shape[2]
    live = lax.broadcasted_iota(jnp.int32, (rows, block), 0) < len_ref[relay]

    @pl.when(step == 0)
    def _():
        acc_ref[...] = jnp.zeros_like(acc_ref)

    odd, high = me % 2 == 1, me // 2 == 1

    def put(kind, i, value):
        value = value.astype(jnp.bfloat16)
        p = [value[q * piece:(q + 1) * piece] for q in range(4)]
        even = [jnp.where(odd, p[k + 1], p[k]) for k in (0, 2)]
        other = [jnp.where(odd, p[k], p[k + 1]) for k in (0, 2)]
        for slot, pair in ((0, even), (1, other)):
            slot_refs[slot][kind, i] = jnp.where(high, pair[1], pair[0])
            slot_refs[slot + 2][kind, i] = jnp.where(high, pair[0], pair[1])

    f32 = jnp.float32
    over_last = (((1,), (1,)), ((), ()))
    over_rows = (((0,), (0,)), ((), ()))
    for start in range(0, per_step, GROUP):
        group = range(start, min(start + GROUP, per_step))
        sources = [idx_in_ref[0, relay, step * per_step + i] for i in group]
        targets = [idx_out_ref[0, relay, step * per_step + i] for i in group]
        picked = [x_ref[:, pl.ds(pl.multiple_of(b * block, block), block)] for b in sources]
        back = [g_ref[:, pl.ds(pl.multiple_of(b * block, block), block)] for b in targets]
        back = [jnp.where(live, v, jnp.zeros_like(v)) for v in back]
        pre = [jnp.dot(v, w_in_ref[i], preferred_element_type=f32) for v, i in zip(picked, group)]
        back_pre = [lax.dot_general(v, w_out_ref[i], over_last, preferred_element_type=f32) for v, i in zip(back, group)]
        act, grad_pre = [], []
        for v, up in zip(pre, back_pre):
            square = v * v
            th = jnp.tanh(SCALE * (v + CUBIC * (square * v)))
            cdf = 0.5 * (1.0 + th)
            act.append((v * cdf).astype(jnp.bfloat16))
            slope = cdf + (0.5 * v) * ((1.0 - th) * (1.0 + th)) * (SCALE * (1.0 + (3.0 * CUBIC) * square))
            grad_pre.append((up * slope).astype(jnp.bfloat16))
        terms = [lax.dot_general(v, w_in_ref[i], over_last, preferred_element_type=f32) for v, i in zip(grad_pre, group)]
        grad_in = [lax.dot_general(a, v, over_rows, preferred_element_type=f32) for a, v in zip(picked, grad_pre)]
        grad_out = [lax.dot_general(a, v, over_rows, preferred_element_type=f32) for a, v in zip(act, back)]
        for i, b, term, g_in, g_out in zip(group, sources, terms, grad_in, grad_out):
            acc_ref[b] += term
            put(0, i, g_in)
            put(1, i, g_out)

    @pl.when(step == pl.num_programs(0) - 1)
    def _():
        share = rows // n_mp
        owned = live & (lax.broadcasted_iota(jnp.int32, (rows, block), 0) // share == lax.axis_index("mp"))
        for b in range(acc_ref.shape[0]):
            columns = slice(b * block, (b + 1) * block)
            held = g_ref[:, columns]
            held = jnp.where(owned, held, jnp.zeros_like(held)).astype(jnp.float32)
            share_ref[:, columns] = (acc_ref[b] + held).astype(jnp.bfloat16)


def tick(relay, sections, n_dp, n_mp, deps, lengths, idx_in, idx_out, section_in, out_grad, w_in, w_out):
    rows, width = section_in.shape[2:]
    blocks, block = w_in.shape[2:4]
    per = blocks // sections
    per_step = math.gcd(per, 24)
    turns = per // per_step
    piece = block // n_dp
    whole = pl.BlockSpec((None, None, rows, width), lambda i, *_: (relay, 0, 0, 0))
    weight = pl.BlockSpec((None, None, per_step, block, block), lambda i, *_: (0, relay, i, 0, 0))
    slots = jax.ShapeDtypeStruct((sections, 2, per, piece, block), jnp.bfloat16)
    slots_spec = pl.BlockSpec((None, 2, per_step, piece, block), lambda i, *_: (i // turns, 0, i % turns, 0, 0))
    return pl.pallas_call(
        functools.partial(tick_kernel, relay, per_step, n_mp, len(deps)),
        grid_spec=pltpu.PrefetchScalarGridSpec(
            num_scalar_prefetch=3,
            grid=(sections * turns,),
            in_specs=[whole, whole, weight, weight] + [pl.BlockSpec(memory_space=pl.ANY)] * len(deps),
            out_specs=[slots_spec] * 4 + [pl.BlockSpec((rows, width), lambda i, *_: (0, 0))],
            scratch_shapes=[pltpu.VMEM((width // block, rows, block), jnp.float32)],
        ),
        out_shape=[slots] * 4 + [jax.ShapeDtypeStruct((rows, width), jnp.bfloat16)],
        compiler_params=pltpu.CompilerParams(
            dimension_semantics=("arbitrary",), vmem_limit_bytes=56 * 1024 * 1024
        ),
        cost_estimate=pl.CostEstimate(
            flops=blocks * 10 * rows * block * block,
            bytes_accessed=blocks * block * block * 8 + rows * width * 6,
            transcendentals=blocks * rows * block,
        ),
        name=f"tick{relay}",
    )(lengths, idx_in, idx_out, section_in, out_grad, w_in, w_out, *deps)


def total(*parts):
    return functools.reduce(lambda a, b: a + b, [p.astype(jnp.float32) for p in parts])


def tie(value, *deps):
    any_space = pl.BlockSpec(memory_space=pl.ANY)
    return pl.pallas_call(
        lambda *refs: None,
        in_specs=[any_space] * (1 + len(deps)),
        out_specs=any_space,
        out_shape=jax.ShapeDtypeStruct(value.shape, value.dtype),
        input_output_aliases={0: 0},
        cost_estimate=pl.CostEstimate(flops=1000, bytes_accessed=1000, transcendentals=0),
        name="tie",
    )(value, *deps)


def flip_bit(value, axis, bit):
    return lax.ppermute(value, axis, [(i, i ^ bit) for i in range(lax.axis_size(axis))])


def from_behind(value, axis, distance):
    devices = range(lax.axis_size(axis))
    route = [(i - distance, i) for i in devices if i - distance in devices]
    return lax.ppermute(value, axis, route)


def rotate(parts, axis):
    n = lax.axis_size(axis)
    me = lax.axis_index(axis)
    got = []
    for k in range(n):
        part = lax.dynamic_index_in_dim(parts, lax.rem(me + k, n), 0, keepdims=False)
        got.append(part if k == 0 else lax.ppermute(part, axis, [(i, (i + k) % n) for i in range(n)]))
    return got


def by_source(parts, axis):
    n = len(parts)
    me = lax.axis_index(axis)
    stacked = jnp.stack(parts)
    return jnp.stack([lax.dynamic_index_in_dim(stacked, lax.rem(me - k + n, n), 0, keepdims=False) for k in range(n)])


def body(section_in, out_grad, lengths, w_in, w_out, idx_in, idx_out):
    sections, n_dp, n_mp = (lax.axis_size(a) for a in ("section", "dp", "mp"))
    args = (lengths.reshape(2), idx_in, idx_out, section_in, out_grad, w_in, w_out)

    def scatter(share):
        return lax.psum_scatter(share, "mp", scatter_dimension=0, tiled=True)

    a0, s0, a2, s2, share0 = tick(0, sections, n_dp, n_mp, [], *args)
    got0, got2 = flip_bit(s0, "dp", 1), flip_bit(s2, "dp", 1)
    sum0 = total(a2, got2).astype(jnp.bfloat16)
    came0 = flip_bit(sum0, "dp", 2)
    b0, t0, b2, t2, share1 = tick(1, sections, n_dp, n_mp, [sum0], *args)
    hot0, hot2 = flip_bit(t0, "dp", 1), flip_bit(t2, "dp", 1)
    dx0 = scatter(share0)
    sum1 = total(tie(b2, came0), hot2).astype(jnp.bfloat16)
    came1 = flip_bit(sum1, "dp", 2)
    dx1 = scatter(tie(share1, came0))
    moved0 = rotate(total(a0, got0, came0).astype(jnp.bfloat16), "section")
    passed0 = from_behind(dx0, "section", -1)
    passed1 = from_behind(dx1, "section", 1)
    moved1 = rotate(total(b0, hot0, came1).astype(jnp.bfloat16), "section")
    grads = total(by_source(moved0, "section"), jnp.flip(by_source(moved1, "section"), 0))
    return jnp.stack([passed0, passed1], axis=0)[:, None], grads[:, :, None]


def solution(mesh):
    placed = (
        P(None, "section", "dp", None),
        P(None, "section", "dp", None),
        P(None, "section", "dp"),
        P("section", None, "mp", None, None),
        P("section", None, "mp", None, None),
        P("section", None, "mp"),
        P("section", None, "mp"),
    )
    return jax.shard_map(
        body,
        mesh=mesh,
        in_specs=placed,
        out_specs=(
            P(None, "section", ("dp", "mp"), None),
            P(None, None, "mp", "section", "dp", None),
        ),
        check_vma=False,
    )
```
